32 devices in a mesh: row: 8 (over z, core), col: 4 (over y, x).
Axes of the slice: x: 2, y: 2, z: 4, core: 2. Of those that a mesh axis runs over, the one named last changes fastest.
Arguments:
- pair: bfloat16 [8, 384, 384, 128], P(None, 'row', 'col'), may hold values from -6 to 6
- cotangent: bfloat16 [8, 384, 384, 128], P(None, 'row', 'col'), may hold values from -6 to 6
- residue_mask: int32 [8, 384], replicated, may hold values 0 or 1
- weights: float32 [6, 128, 128], replicated, may hold values from -0.5 to 0.5
- norm_params: float32 [4, 128], replicated, may hold values from 0.1 to 1.9
- momentum: float32 [6, 128, 128], replicated, may hold values from -320 to 320
- norm_momentum: float32 [4, 128], replicated, may hold values from -320 to 320
- average: float32 [6, 128, 128], replicated, may hold values from -0.5 to 0.5
- norm_average: float32 [4, 128], replicated, may hold values from 0.1 to 1.9
Outputs:
- new_pair: bfloat16 [8, 384, 384, 128], P(None, 'row', 'col')
- pair_grad: bfloat16 [8, 384, 384, 128], P(None, 'row', 'col')
- new_weights: float32 [6, 128, 128], replicated
- new_momentum: float32 [6, 128, 128], replicated
- new_average: float32 [6, 128, 128], replicated
- new_norms: float32 [4, 128], replicated
- new_norm_momentum: float32 [4, 128], replicated
- new_norm_average: float32 [4, 128], replicated
The draws below stay inside these ranges and needn't reach their ends.
All inputs are finite; a program needn't handle non-finite values.
Results may differ from the reference program's by a relative error of at most 0.0089.
Values may be sent and summed in bfloat16 or wider, within the bound.
No kernel may reach another device: no remote copies, remote signals or barrier semaphores. Data moves between devices by JAX's collectives and lax.ppermute only.
A program may use at most 192 MiB of HBM per device.

```python
import math
import jax
import jax.numpy as jnp
from jax import lax

C = 128
L = 384
CROPS = 8


def plant(entries, stream_key, low, high):
    index_at = [jax.random.randint(jax.random.fold_in(stream_key, axis), (), 0, length) for axis, length in enumerate(entries.shape)]
    main_axis = entries.shape.index(max(entries.shape))
    beside = index_at[:main_axis] + [(index_at[main_axis] + 1) % entries.shape[main_axis]] + index_at[main_axis + 1:]
    return entries.at[tuple(index_at)].set(low).at[tuple(beside)].set(high)


def block_scale(key, dims, split, least, largest):
    factor_of, own = 1.0, jax.random.fold_in(key, 6)
    for position, blocks in split:
        draws = jnp.exp(jax.random.uniform(jax.random.fold_in(own, position), (blocks,), jnp.float32, least / len(split), largest / len(split)))
        factor_of = factor_of * jnp.repeat(draws, dims[position] // blocks).reshape([-1 if axis == position else 1 for axis in range(len(dims))])
    return factor_of


def bell_draw(rng, dims, width, most, shards=(), held_as=jnp.bfloat16):
    drawn = jax.random.normal(rng, dims, jnp.float32) * width
    if len(shards) > 0:
        drawn = block_scale(rng, dims, shards, -0.22, 0.18) * drawn
    return jnp.clip(drawn, min=-most, max=most).astype(held_as)


def setup_inputs(seed: int = 0) -> dict:
    key_of = jax.random.split(jax.random.key(seed), 10)
    pair = bell_draw(key_of[0], (CROPS, L, L, C), 1.0, 6.0, ((1, 8), (2, 4)))
    cotangent = bell_draw(key_of[1], (CROPS, L, L, C), 1.0, 6.0, ((1, 8), (2, 4)))
    residue_mask = plant((jax.random.randint(key_of[2], (CROPS, L), 0, 8) < 7).astype(jnp.int32), jax.random.fold_in(key_of[2], 1), 0, 1)
    weights = bell_draw(key_of[3], (6, C, C), C ** -0.5, 0.5, (), jnp.float32)
    norm_params = jnp.clip(1.0 + 0.18 * jax.random.normal(key_of[4], (4, C), jnp.float32), 0.1, 1.9)
    momentum = bell_draw(key_of[5], (6, C, C), (0.05 * L * CROPS ** 0.5), 320.0, (), jnp.float32)
    norm_momentum = bell_draw(key_of[6], (4, C), (0.05 * L * CROPS ** 0.5), 320.0, (), jnp.float32)
    average = bell_draw(key_of[7], (6, C, C), C ** -0.5, 0.5, (), jnp.float32)
    norm_average = jnp.clip(1.0 + 0.18 * jax.random.normal(key_of[8], (4, C), jnp.float32), 0.1, 1.9)
    return {"pair": pair, "cotangent": cotangent, "residue_mask": residue_mask, "weights": weights, "norm_params": norm_params, "momentum": momentum, "norm_momentum": norm_momentum, "average": average, "norm_average": norm_average}


EPS = 1e-05
MOMENT = 0.9
DECAY = 0.8
HIGH = lax.Precision.HIGHEST

@jax.custom_vjp
def low(v):
    return lax.optimization_barrier(v.astype(jnp.bfloat16)).astype(jnp.float32)

@jax.custom_vjp
def low_back(v):
    return v

def low_keep(v):
    return (low(v), None)

def low_pass(kept, grad):
    return (grad,)

def back_keep(v):
    return (v, None)

def back_low(kept, grad):
    return (low(grad),)
low.defvjp(low_keep, low_pass)
low_back.defvjp(back_keep, back_low)

def normalize(field):
    center = field - lax.optimization_barrier(jnp.mean(field, axis=-1, keepdims=True))
    return center * lax.rsqrt(lax.optimization_barrier(jnp.mean(center * center, axis=-1, keepdims=True)) + EPS)

def crop_forward(pair_crop, mask_crop, weight_arg, norm_arg):
    inner = low(normalize(pair_crop) * norm_arg[0] + norm_arg[1])
    weight_low = low(weight_arg)
    project = low_back(jnp.einsum('ijc,ncd->nijd', inner, weight_low[:5], precision=HIGH))
    mask_float = mask_crop.astype(jnp.float32)
    pair_mask = (mask_float[:, None] * mask_float[None, :])[:, :, None]
    left_edge = low(jax.nn.sigmoid(project[1]) * project[0] * pair_mask)
    right_edge = low(jax.nn.sigmoid(project[3]) * project[2] * pair_mask)
    product = low_back(jnp.einsum('ikc,jkc->ijc', left_edge, right_edge, precision=HIGH))
    mixed = low(normalize(product) * norm_arg[2] + norm_arg[3])
    output = low_back(jnp.einsum('ijc,cd->ijd', mixed, weight_low[5], precision=HIGH))
    return pair_crop + jax.nn.sigmoid(project[4]) * output

def reference(pair, cotangent, residue_mask, weights, norm_params, momentum, norm_momentum, average, norm_average):
    pair_float = pair.astype(jnp.float32)
    cot_float = cotangent.astype(jnp.float32)

    def forward(weight_arg, norm_arg, pair_arg):

        def one_crop(items):
            return crop_forward(items[0], items[1], weight_arg, norm_arg)
        return lax.map(jax.checkpoint(one_crop), (pair_arg, residue_mask))
    new_pair, pullback = jax.vjp(forward, weights, norm_params, pair_float)
    grad_weights, grad_norms, grad_pair = pullback(cot_float)
    rate = 0.1 / (L * math.sqrt(CROPS))
    new_momentum = MOMENT * momentum + grad_weights
    new_weights = weights - rate * (grad_weights + MOMENT * new_momentum)
    new_average = DECAY * average + (1.0 - DECAY) * new_weights
    new_norm_momentum = MOMENT * norm_momentum + grad_norms
    new_norms = norm_params - rate * (grad_norms + MOMENT * new_norm_momentum)
    new_norm_average = DECAY * norm_average + (1.0 - DECAY) * new_norms
    return (new_pair.astype(jnp.bfloat16), grad_pair.astype(jnp.bfloat16), new_weights, new_momentum, new_average, new_norms, new_norm_momentum, new_norm_average)
```

```python
import math

import jax
import jax.numpy as jnp
from jax import lax
from jax.experimental import pallas as pl
from jax.experimental.pallas import tpu as pltpu
from jax.sharding import PartitionSpec as P

EPS = 1e-05
MOMENT = 0.9
DECAY = 0.8
LOW = jnp.bfloat16
F32 = jnp.float32
MIB = 1 << 20
COST = 1.0


def sds(shape, dtype):
    return jax.ShapeDtypeStruct(shape, dtype)


def params(mib):
    return pltpu.CompilerParams(vmem_limit_bytes=mib * MIB)


def cost(flops, moved):
    return pl.CostEstimate(flops=int(flops * COST), bytes_accessed=int(moved * COST),
                           transcendentals=0)


def sigmoid(v):
    return 0.5 * jnp.tanh(0.5 * v) + 0.5


def normalize(v):
    center = v - jnp.mean(v, axis=-1, keepdims=True)
    inverse = lax.rsqrt(jnp.mean(center * center, axis=-1, keepdims=True) + EPS)
    return center * inverse, inverse


def norm_back(grad_hat, normed, inverse):
    first = jnp.mean(grad_hat, axis=-1, keepdims=True)
    second = jnp.mean(grad_hat * normed, axis=-1, keepdims=True)
    return inverse * (grad_hat - first - normed * second)


def dot(a, b, ca=1, cb=0):
    return lax.dot_general(a, b, (((ca,), (cb,)), ((), ())), preferred_element_type=F32)


def eights(v):
    return jnp.sum(v.reshape(-1, 8, v.shape[-1]), axis=0)


def to_major(v):
    return jnp.swapaxes(jnp.swapaxes(v, 1, 2), 0, 1)


def to_minor(v):
    return jnp.swapaxes(jnp.swapaxes(v, 0, 1), 1, 2)


def row_mask(rowm, colm, start, count):
    m = rowm[pl.ds(start, count)][:, None, :] * colm[...][None]
    return m.reshape(-1, m.shape[-1])


def pick_rows(nrow):
    return 16 if nrow % 16 == 0 else 8


def fold(nblocks, refs, dst):
    for d in range(nblocks):
        @pl.when(pl.program_id(0) == d)
        def _(d=d):
            dst[...] = refs[d][...]


def clamp_map(d, steps):
    def index(g, r, *_):
        return (jnp.where(g == d, r, jnp.where(g < d, 0, steps - 1)), 0, 0)
    return index


def edges_kernel(nblocks, sub, *refs):
    zs, (norms, proj, rowm, colm, left, right, tile) = refs[:nblocks], refs[nblocks:]
    rows, nk, chan = tile.shape
    fold(nblocks, zs, tile)
    base = (pl.program_id(0) * pl.num_programs(1) + pl.program_id(1)) * rows

    def step(t, _):
        at = t * sub
        z = tile[pl.ds(at, sub)].astype(F32).reshape(-1, chan)
        hat, _ = normalize(z)
        u = (hat * norms[0:1] + norms[1:2]).astype(LOW)
        p = dot(u, proj[...])
        m = row_mask(rowm, colm, base + at, sub)
        lv = sigmoid(p[:, chan:2 * chan]) * p[:, :chan] * m
        rv = sigmoid(p[:, 3 * chan:]) * p[:, 2 * chan:3 * chan] * m
        left[pl.ds(at, sub)] = lv.astype(LOW).reshape(sub, nk, chan)
        right[pl.ds(at, sub)] = rv.astype(LOW).reshape(sub, nk, chan)
        return 0

    lax.fori_loop(0, rows // sub, step, 0)


def edges_call(zs, norms, proj, rowm, colm):
    nblocks = len(zs)
    nrow, nk, chan = zs[0].shape
    rows = pick_rows(nrow)
    steps = nrow // rows
    whole = lambda shape: pl.BlockSpec(shape, lambda g, r: (0,) * len(shape))
    flat = pl.BlockSpec((rows, nk, chan), lambda g, r: (g * steps + r, 0, 0))
    cells = nblocks * nrow * nk
    return pl.pallas_call(
        lambda *refs: edges_kernel(nblocks, 4, *refs),
        grid=(nblocks, steps),
        in_specs=[pl.BlockSpec((rows, nk, chan), clamp_map(d, steps)) for d in range(nblocks)]
        + [whole(norms.shape), whole(proj.shape), whole(rowm.shape), whole(colm.shape)],
        out_specs=[flat, flat],
        out_shape=[sds((nblocks * nrow, nk, chan), LOW)] * 2,
        scratch_shapes=[pltpu.VMEM((rows, nk, chan), LOW)],
        compiler_params=params(32),
        cost_estimate=cost(cells * chan * chan * 8, cells * chan * 6),
        name="edges",
    )(*zs, norms, proj, rowm, colm)


def product_kernel(nparts, unroll, sc, left, own, other, *refs):
    outs, (lt, rt, xt) = refs[:nparts], refs[nparts:]
    s = pl.program_id(0)
    rows, nk, chan = left.shape
    chunk = pick_rows(rows)
    half = nparts * rows
    core = sc[0]

    @pl.when(s < nparts)
    def _():
        def move(t, _):
            at = pl.multiple_of(t * chunk, chunk)
            to = s * rows + at
            lt[:, pl.ds(pl.multiple_of(to, chunk), chunk), :] = to_major(left[pl.ds(at, chunk)])
            rt[:, pl.ds(pl.multiple_of(core * half + to, chunk), chunk), :] = to_major(
                own[0, pl.ds(at, chunk)])
            rt[:, pl.ds(pl.multiple_of((1 - core) * half + to, chunk), chunk), :] = to_major(
                other[0, pl.ds(at, chunk)])
            return 0
        lax.fori_loop(0, rows // chunk, move, 0)

    @pl.when(s == nparts)
    def _():
        def multiply(c, _):
            xt[c] = dot(lt[c], rt[c], 1, 1).astype(LOW)
            return 0
        lax.fori_loop(0, chan, multiply, 0, unroll=unroll)

    @pl.when(s >= nparts)
    def _():
        def move(t, _):
            at = pl.multiple_of(t * chunk, chunk)
            x = to_minor(xt[:, pl.ds(pl.multiple_of((s - nparts) * rows + at, chunk), chunk), :])
            for e in range(nparts):
                for core in range(2):
                    start = core * half + e * rows
                    outs[e][pl.ds(at, chunk), core * rows:(core + 1) * rows] = (
                        x[:, start:start + rows])
            return 0
        lax.fori_loop(0, rows // chunk, move, 0)


def product_call(scal, left, own, other):
    nparts, rows, nk, chan = own.shape
    ni, nj = nparts * rows, 2 * nparts * rows
    last = nparts - 1
    edge = pl.BlockSpec((1, rows, nk, chan),
                        lambda s, sc: (sc[1 + jnp.minimum(s, last)], 0, 0, 0))
    return pl.pallas_call(
        lambda *refs: product_kernel(nparts, 4, *refs),
        grid_spec=pltpu.PrefetchScalarGridSpec(
            num_scalar_prefetch=1,
            grid=(2 * nparts,),
            in_specs=[pl.BlockSpec((rows, nk, chan), lambda s, sc: (jnp.minimum(s, last), 0, 0)),
                      edge, edge],
            out_specs=[pl.BlockSpec((rows, 2 * rows, chan),
                                    lambda s, sc: (jnp.maximum(s - nparts, 0), 0, 0))] * nparts,
            scratch_shapes=[pltpu.VMEM((chan, ni, nk), LOW), pltpu.VMEM((chan, nj, nk), LOW),
                            pltpu.VMEM((chan, ni, nj), LOW)],
        ),
        out_shape=[sds((ni, 2 * rows, chan), LOW)] * nparts,
        compiler_params=params(60),
        cost_estimate=cost(2 * ni * nj * nk * chan * 8, 14 * ni * nk * chan),
        name="product",
    )(scal, left, own, other)


def middle_kernel(nblocks, nparts, sub, *refs):
    zs, refs = refs[:nblocks], refs[nblocks:]
    gs, refs = refs[:nblocks], refs[nblocks:]
    xs, refs = refs[:nparts], refs[nparts:]
    (norms, gate_w, out_w), refs = refs[:3], refs[3:]
    news, refs = refs[:nblocks], refs[nblocks:]
    gx, gate_grad, wout, nout, ztile, gtile, ntile, ylow, glow = refs
    rows, nk, chan = ztile.shape
    fold(nblocks, zs, ztile)
    fold(nblocks, gs, gtile)

    @pl.when((pl.program_id(0) == 0) & (pl.program_id(1) == 0))
    def _():
        wout[...] = jnp.zeros_like(wout)
        nout[...] = jnp.zeros_like(nout)

    def step(t, _):
        rng = pl.ds(t * sub, sub)
        flat = pl.ds(pl.multiple_of(t * sub * nk, sub * nk), sub * nk)
        z = ztile[rng].astype(F32).reshape(-1, chan)
        zhat, _ = normalize(z)
        u = (zhat * norms[0:1] + norms[1:2]).astype(LOW)
        gate = sigmoid(dot(u, gate_w[...]))
        x = xs[0][rng].astype(F32)
        for other in xs[1:]:
            x = x + other[rng].astype(F32)
        hat, inverse = normalize(x.reshape(-1, chan))
        y = (hat * norms[2:3] + norms[3:4]).astype(LOW)
        out = dot(y, out_w[...])
        so = gate * out
        ntile[rng] = (z + so).astype(LOW).reshape(sub, nk, chan)
        g = gtile[rng].astype(F32).reshape(-1, chan)
        go = (g * gate).astype(LOW)
        gate_grad[rng] = (g * so * (1.0 - gate)).astype(LOW).reshape(sub, nk, chan)
        ylow[flat] = y
        glow[flat] = go
        gy = dot(go, out_w[...], 1, 1)
        nout[0] += eights(gy * hat)
        nout[1] += eights(gy)
        gx[rng] = norm_back(gy * norms[2:3], hat, inverse).astype(LOW).reshape(sub, nk, chan)
        return 0

    lax.fori_loop(0, rows // sub, step, 0)
    wout[...] += dot(ylow[...], glow[...], 0, 0)
    for d in range(nblocks):
        @pl.when(pl.program_id(0) == d)
        def _(d=d):
            news[d][...] = ntile[...]


def middle_call(zs, gs, xs, norms, gate_w, out_w):
    nblocks, nparts = len(zs), len(xs)
    nrow, nk, chan = zs[0].shape
    rows = pick_rows(nrow)
    steps = nrow // rows
    whole = lambda shape: pl.BlockSpec(shape, lambda g, r: (0,) * len(shape))
    flat = pl.BlockSpec((rows, nk, chan), lambda g, r: (g * steps + r, 0, 0))
    block = [pl.BlockSpec((rows, nk, chan), clamp_map(d, steps)) for d in range(nblocks)]
    cells = nblocks * nrow * nk
    tile = pltpu.VMEM((rows, nk, chan), LOW)
    low = pltpu.VMEM((rows * nk, chan), LOW)
    return pl.pallas_call(
        lambda *refs: middle_kernel(nblocks, nparts, 4, *refs),
        grid=(nblocks, steps),
        in_specs=block + block + [flat] * nparts
        + [whole(norms.shape), whole(gate_w.shape), whole(out_w.shape)],
        out_specs=block + [flat, flat, whole((chan, chan)), whole((2, 8, chan))],
        out_shape=[sds((nrow, nk, chan), LOW)] * nblocks
        + [sds((nblocks * nrow, nk, chan), LOW)] * 2
        + [sds((chan, chan), F32), sds((2, 8, chan), F32)],
        scratch_shapes=[tile, tile, tile, low, low],
        compiler_params=params(40),
        cost_estimate=cost(cells * chan * chan * 8, cells * chan * 18),
        name="middle",
    )(*zs, *gs, *xs, norms, gate_w, out_w)


def edge_grad_kernel(nparts, unroll, sc, left, own, other, *refs):
    gxs, (gleft, keep, send, lt, rt, gt) = refs[:nparts], refs[nparts:]
    s = pl.program_id(0)
    rows, nk, chan = left.shape
    chunk = pick_rows(rows)
    half = nparts * rows
    core = sc[0]

    @pl.when(s < nparts)
    def _():
        def move(t, _):
            at = pl.multiple_of(t * chunk, chunk)
            to = s * rows + at
            to_l = pl.multiple_of(to, chunk)
            lt[:, pl.ds(to_l, chunk), :] = to_major(left[pl.ds(at, chunk)])
            rt[:, pl.ds(pl.multiple_of(core * half + to, chunk), chunk), :] = to_major(
                own[0, pl.ds(at, chunk)])
            rt[:, pl.ds(pl.multiple_of((1 - core) * half + to, chunk), chunk), :] = to_major(
                other[0, pl.ds(at, chunk)])
            g = jnp.concatenate([
                gxs[e][pl.ds(at, chunk), c * rows:(c + 1) * rows]
                for c in range(2) for e in range(nparts)
            ], axis=1)
            gt[:, pl.ds(to_l, chunk), :] = to_major(g)
            return 0
        lax.fori_loop(0, rows // chunk, move, 0)

    @pl.when(s == nparts)
    def _():
        def multiply(c, _):
            lc, rc, gc = lt[c], rt[c], gt[c]
            lt[c] = dot(gc, rc, 1, 0).astype(LOW)
            rt[c] = dot(gc, lc, 0, 0).astype(LOW)
            return 0
        lax.fori_loop(0, chan, multiply, 0, unroll=unroll)

    @pl.when(s >= nparts)
    def _():
        def move(t, _):
            at = pl.multiple_of(t * chunk, chunk)
            to = (s - nparts) * rows + at
            gleft[pl.ds(at, chunk)] = to_minor(lt[:, pl.ds(pl.multiple_of(to, chunk), chunk), :])
            keep[0, pl.ds(at, chunk)] = to_minor(
                rt[:, pl.ds(pl.multiple_of(core * half + to, chunk), chunk), :])
            send[0, pl.ds(at, chunk)] = to_minor(
                rt[:, pl.ds(pl.multiple_of((1 - core) * half + to, chunk), chunk), :])
            return 0
        lax.fori_loop(0, rows // chunk, move, 0)


def edge_grad_call(scal, left, own, other, gxs):
    nparts, rows, nk, chan = own.shape
    ni, nj = nparts * rows, 2 * nparts * rows
    last = nparts - 1
    edge = pl.BlockSpec((1, rows, nk, chan),
                        lambda s, sc: (sc[1 + jnp.minimum(s, last)], 0, 0, 0))
    back = pl.BlockSpec((1, rows, nk, chan),
                        lambda s, sc: (sc[1 + jnp.maximum(s - nparts, 0)], 0, 0, 0))
    first = lambda s, sc: (jnp.minimum(s, last), 0, 0)
    return pl.pallas_call(
        lambda *refs: edge_grad_kernel(nparts, 4, *refs),
        grid_spec=pltpu.PrefetchScalarGridSpec(
            num_scalar_prefetch=1,
            grid=(2 * nparts,),
            in_specs=[pl.BlockSpec((rows, nk, chan), first), edge, edge]
            + [pl.BlockSpec((rows, 2 * rows, chan), first)] * nparts,
            out_specs=[pl.BlockSpec((rows, nk, chan),
                                    lambda s, sc: (jnp.maximum(s - nparts, 0), 0, 0)), back, back],
            scratch_shapes=[pltpu.VMEM((chan, ni, nk), LOW), pltpu.VMEM((chan, nj, nk), LOW),
                            pltpu.VMEM((chan, ni, nj), LOW)],
        ),
        out_shape=[sds((ni, nk, chan), LOW), sds((nparts, rows, nk, chan), LOW),
                   sds((nparts, rows, nk, chan), LOW)],
        compiler_params=params(62),
        cost_estimate=cost(4 * ni * nj * nk * chan * 8, 14 * ni * nk * chan),
        name="edge_grad",
    )(scal, left, own, other, *gxs)


def input_kernel(nblocks, sub, *refs):
    zs, refs = refs[:nblocks], refs[nblocks:]
    gs, refs = refs[:nblocks], refs[nblocks:]
    (gleft, keep, got, gate_grad, norms, proj, rowm, colm), refs = refs[:8], refs[8:]
    outs, refs = refs[:nblocks], refs[nblocks:]
    wproj, nin, ztile, gtile, otile, ulow, plow = refs
    rows, nk, chan = ztile.shape
    fold(nblocks, zs, ztile)
    fold(nblocks, gs, gtile)
    base = (pl.program_id(0) * pl.num_programs(1) + pl.program_id(1)) * rows

    @pl.when((pl.program_id(0) == 0) & (pl.program_id(1) == 0))
    def _():
        wproj[...] = jnp.zeros_like(wproj)
        nin[...] = jnp.zeros_like(nin)

    def step(t, _):
        at = t * sub
        rng = pl.ds(at, sub)
        flat = pl.ds(pl.multiple_of(at * nk, sub * nk), sub * nk)
        z = ztile[rng].astype(F32).reshape(-1, chan)
        hat, inverse = normalize(z)
        u = (hat * norms[0:1] + norms[1:2]).astype(LOW)
        ulow[flat] = u
        p = dot(u, proj[:, :4 * chan])
        m = row_mask(rowm, colm, base + at, sub)
        gl = gleft[rng].astype(F32).reshape(-1, chan) * m
        gr = (keep[rng].astype(F32) + got[rng].astype(F32)).reshape(-1, chan) * m
        for n, grad in ((0, gl), (2, gr)):
            sig = sigmoid(p[:, (n + 1) * chan:(n + 2) * chan])
            first = grad * sig
            plow[flat, n * chan:(n + 1) * chan] = first.astype(LOW)
            second = first * (p[:, n * chan:(n + 1) * chan] * (1.0 - sig))
            plow[flat, (n + 1) * chan:(n + 2) * chan] = second.astype(LOW)
        plow[flat, 4 * chan:] = gate_grad[rng].reshape(-1, chan)
        gu = dot(plow[flat], proj[...], 1, 1)
        nin[0] += eights(gu * hat)
        nin[1] += eights(gu)
        g = gtile[rng].astype(F32).reshape(-1, chan)
        grad_z = g + norm_back(gu * norms[0:1], hat, inverse)
        otile[rng] = grad_z.astype(LOW).reshape(sub, nk, chan)
        return 0

    lax.fori_loop(0, rows // sub, step, 0)
    wproj[...] += dot(ulow[...], plow[...], 0, 0)
    for d in range(nblocks):
        @pl.when(pl.program_id(0) == d)
        def _(d=d):
            outs[d][...] = otile[...]


def input_call(zs, gs, gleft, keep, got, gate_grad, norms, proj, rowm, colm):
    nblocks = len(zs)
    nrow, nk, chan = zs[0].shape
    rows = pick_rows(nrow)
    steps = nrow // rows
    whole = lambda shape: pl.BlockSpec(shape, lambda g, r: (0,) * len(shape))
    flat = pl.BlockSpec((rows, nk, chan), lambda g, r: (g * steps + r, 0, 0))
    block = [pl.BlockSpec((rows, nk, chan), clamp_map(d, steps)) for d in range(nblocks)]
    cells = nblocks * nrow * nk
    width = proj.shape[1]
    tile = pltpu.VMEM((rows, nk, chan), LOW)
    return pl.pallas_call(
        lambda *refs: input_kernel(nblocks, 4, *refs),
        grid=(nblocks, steps),
        in_specs=block + block + [flat] * 4
        + [whole(norms.shape), whole(proj.shape), whole(rowm.shape), whole(colm.shape)],
        out_specs=block + [whole((chan, width)), whole((2, 8, chan))],
        out_shape=[sds((nrow, nk, chan), LOW)] * nblocks
        + [sds((chan, width), F32), sds((2, 8, chan), F32)],
        scratch_shapes=[tile, tile, tile, pltpu.VMEM((rows * nk, chan), LOW),
                        pltpu.VMEM((rows * nk, width), LOW)],
        compiler_params=params(40),
        cost_estimate=cost(cells * chan * chan * 28, cells * chan * 14),
        name="input_grad",
    )(*zs, *gs, gleft, keep, got, gate_grad, norms, proj, rowm, colm)


def place_call(scal, pieces, whole=None, shape=None):
    count = len(pieces)
    fresh = whole is None
    nrow, nk, chan = pieces[0].shape
    rows = pick_rows(nrow)
    steps = nrow // rows

    def kernel(*refs):
        blocks, out = refs[1:1 + count], refs[-1]
        for n in range(count):
            @pl.when(pl.program_id(0) == n)
            def _(n=n):
                out[0] = blocks[n][...]

    args = [scal, *pieces] + ([] if fresh else [whole])
    return pl.pallas_call(
        kernel,
        grid_spec=pltpu.PrefetchScalarGridSpec(
            num_scalar_prefetch=1,
            grid=(count, steps),
            in_specs=[pl.BlockSpec((rows, nk, chan), clamp_map(n, steps)) for n in range(count)]
            + [pl.BlockSpec(memory_space=pl.ANY)] * (0 if fresh else 1),
            out_specs=pl.BlockSpec((1, rows, nk, chan), lambda g, r, sc: (sc[g], r, 0, 0)),
        ),
        out_shape=sds(shape if fresh else whole.shape, LOW),
        input_output_aliases={} if fresh else {len(args) - 1: 0},
        compiler_params=params(32),
        cost_estimate=cost(0, 4 * count * nrow * nk * chan),
        name="place",
    )(*args)


def shards(rows, cols, pair, cotangent, residue_mask, weights, norm_params, momentum,
           norm_momentum, average, norm_average):
    zeds = rows // 2
    crops, nrow, ncol, chan = pair.shape
    batches = crops // zeds
    length = residue_mask.shape[1]
    row = lax.axis_index("row")
    col = lax.axis_index("col")
    zed, core = row // 2, row % 2
    weight_low = weights.astype(LOW)
    project_low = jnp.concatenate([weight_low[n] for n in range(5)], axis=1)
    mask_float = residue_mask.astype(F32)
    scal = jnp.stack([core] + [zed ^ col ^ e for e in range(cols)]).astype(jnp.int32)

    def zswap(block, d):
        if d == 0:
            return block
        return lax.ppermute(block, "row", [(r, r ^ (2 * d)) for r in range(rows)])

    def cswap(block, e):
        if e == 0:
            return block
        return lax.ppermute(block, "col", [(q, q ^ e) for q in range(cols)])

    def coreswap(block):
        return lax.ppermute(block, "row", [(r, r ^ 1) for r in range(rows)])

    def fetch(whole, b):
        return [
            zswap(lax.dynamic_index_in_dim(whole, (zed ^ d) * batches + b, 0, keepdims=False), d)
            for d in range(zeds)
        ]

    def blocked(v):
        return v.reshape(zeds, nrow, ncol, chan)

    masks = []
    for b in range(batches):
        crop_mask = lax.dynamic_index_in_dim(mask_float, zed * batches + b, 0, keepdims=False)
        rowm = jnp.concatenate([
            lax.dynamic_slice_in_dim(crop_mask, ((zed ^ d) * 2 + core) * nrow, nrow, 0)
            for d in range(zeds)
        ])
        colm = lax.dynamic_slice_in_dim(crop_mask, col * ncol, ncol, 0)
        masks.append((jnp.broadcast_to(rowm[:, None], (zeds * nrow, chan)),
                      jnp.broadcast_to(colm[:, None], (ncol, chan))))

    pairs = [fetch(pair, b) for b in range(batches)]
    cots = [fetch(cotangent, b) for b in range(batches)]
    lefts, owns, others, parts = [], [], [], []
    for b in range(batches):
        left, right = edges_call(pairs[b], norm_params, project_low[:, :4 * chan], *masks[b])
        own = blocked(right)
        other = coreswap(own)
        part = product_call(scal, left, own, other)
        lefts.append(left)
        owns.append(own)
        others.append(other)
        parts.append([cswap(part[e], e) for e in range(cols)])
    news, grads, gates, sums = [], [], [], []
    for b in range(batches):
        out = middle_call(pairs[b], cots[b], parts[b], norm_params, weight_low[4], weight_low[5])
        new, (gx, gate_grad, wout, nout) = out[:zeds], out[zeds:]
        news.append([zswap(new[d], d) for d in range(zeds)])
        grads.append([cswap(gx, e) for e in range(cols)])
        gates.append(gate_grad)
        sums.append((wout, nout))
    backs, flats = [], []
    for b in range(batches):
        gleft, keep, send = edge_grad_call(scal, lefts[b], owns[b], others[b], grads[b])
        got = coreswap(send)
        joined = (zeds * nrow, ncol, chan)
        out = input_call(pairs[b], cots[b], gleft, keep.reshape(joined), got.reshape(joined),
                         gates[b], norm_params, project_low, *masks[b])
        back, (wproj, nin) = out[:zeds], out[zeds:]
        backs.append([zswap(back[d], d) for d in range(zeds)])
        wout, nout = sums[b]
        wproj = jnp.transpose(wproj.reshape(chan, 5, chan), (1, 0, 2)).reshape(5 * chan, chan)
        flats.append(jnp.concatenate(
            [wproj, wout, jnp.sum(nin, axis=1), jnp.sum(nout, axis=1)], axis=0))

    def collect(pieces):
        whole = None
        for b in range(batches):
            where = jnp.stack([(zed ^ d) * batches + b for d in range(zeds)]).astype(jnp.int32)
            whole = place_call(where, pieces[b], whole, pair.shape)
        return whole

    new_pair = collect(news)
    pair_grad = collect(backs)
    flat = lax.psum(sum(flats), ("row", "col"))
    grad_weights = flat[: 6 * chan].reshape(weights.shape)
    grad_norms = flat[6 * chan:]
    rate = 0.1 / (length * math.sqrt(crops))
    new_momentum = MOMENT * momentum + grad_weights
    new_weights = weights - rate * (grad_weights + MOMENT * new_momentum)
    new_average = DECAY * average + (1.0 - DECAY) * new_weights
    new_norm_momentum = MOMENT * norm_momentum + grad_norms
    new_norms = norm_params - rate * (grad_norms + MOMENT * new_norm_momentum)
    new_norm_average = DECAY * norm_average + (1.0 - DECAY) * new_norms
    return (new_pair, pair_grad, new_weights, new_momentum, new_average, new_norms,
            new_norm_momentum, new_norm_average)


def solution(mesh):
    rows, cols = mesh.shape["row"], mesh.shape["col"]
    tiled = P(None, "row", "col", None)

    def body(*args):
        return shards(rows, cols, *args)

    return jax.shard_map(
        body,
        mesh=mesh,
        in_specs=(tiled, tiled) + (P(),) * 7,
        out_specs=(tiled, tiled) + (P(),) * 6,
        check_vma=False,
    )
```

```python
import math

import jax
import jax.numpy as jnp
from jax import lax
from jax.experimental import pallas as pl
from jax.experimental.pallas import tpu as pltpu
from jax.sharding import PartitionSpec as P

EPS = 1e-05
MOMENT = 0.9
DECAY = 0.8
LOW = jnp.bfloat16
F32 = jnp.float32
MIB = 1 << 20
SHARE = 600_000_000


def sds(shape, dtype):
    return jax.ShapeDtypeStruct(shape, dtype)


def params(mib):
    return pltpu.CompilerParams(vmem_limit_bytes=mib * MIB)


def cost(micros):
    return pl.CostEstimate(flops=int(micros * SHARE), bytes_accessed=0, transcendentals=0)


def sigmoid(v):
    return 0.5 * jnp.tanh(0.5 * v) + 0.5


def normalize(v):
    center = v - jnp.mean(v, axis=-1, keepdims=True)
    inverse = lax.rsqrt(jnp.mean(center * center, axis=-1, keepdims=True) + EPS)
    return center * inverse, inverse


def norm_back(grad_hat, normed, inverse):
    first = jnp.mean(grad_hat, axis=-1, keepdims=True)
    second = jnp.mean(grad_hat * normed, axis=-1, keepdims=True)
    return inverse * (grad_hat - first - normed * second)


def dot(a, b, ca=1, cb=0):
    return lax.dot_general(a, b, (((ca,), (cb,)), ((), ())), preferred_element_type=F32)


def eights(v):
    return jnp.sum(v.reshape(-1, 8, v.shape[-1]), axis=0)


def to_major(v):
    return jnp.swapaxes(jnp.swapaxes(v, 1, 2), 0, 1)


def to_minor(v):
    return jnp.swapaxes(jnp.swapaxes(v, 0, 1), 1, 2)


def row_mask(rowm, colm, start, count):
    m = rowm[pl.ds(start, count)][:, None, :] * colm[...][None]
    return m.reshape(-1, m.shape[-1])


def pick_rows(nrow):
    return 16 if nrow % 16 == 0 else 8


def whole_spec(array):
    return pl.BlockSpec(array.shape, lambda s: (0,) * len(array.shape))


def edges_kernel(sub, z_ref, norms, proj, rowm, colm, left, right):
    rows, nk, chan = z_ref.shape
    base = pl.program_id(0) * rows

    def step(t, _):
        at = t * sub
        z = z_ref[pl.ds(at, sub)].astype(F32).reshape(-1, chan)
        hat, _ = normalize(z)
        u = (hat * norms[0:1] + norms[1:2]).astype(LOW)
        p = dot(u, proj[...])
        m = row_mask(rowm, colm, base + at, sub)
        lv = sigmoid(p[:, chan:2 * chan]) * p[:, :chan] * m
        rv = sigmoid(p[:, 3 * chan:]) * p[:, 2 * chan:3 * chan] * m
        left[pl.ds(at, sub)] = lv.astype(LOW).reshape(sub, nk, chan)
        right[pl.ds(at, sub)] = rv.astype(LOW).reshape(sub, nk, chan)
        return 0

    lax.fori_loop(0, rows // sub, step, 0)


def edges_call(z, norms, proj, rowm, colm):
    ni, nk, chan = z.shape
    rows = 16
    flat = pl.BlockSpec((rows, nk, chan), lambda s: (s, 0, 0))
    return pl.pallas_call(
        lambda *refs: edges_kernel(4, *refs),
        grid=(ni // rows,),
        in_specs=[flat] + [whole_spec(v) for v in (norms, proj, rowm, colm)],
        out_specs=[flat, flat],
        out_shape=[sds(z.shape, LOW)] * 2,
        compiler_params=params(32),
        cost_estimate=cost(27),
        name="edges",
    )(z, norms, proj, rowm, colm)


def product_kernel(nparts, unroll, sc, left, own, other, out, lt, rt, xt):
    s = pl.program_id(0)
    steps = pl.num_programs(0) // 2
    rows, nk, chan = left.shape
    nrow = out.shape[2] // 2
    half = nparts * nrow
    core = sc[0]

    @pl.when(s < steps)
    def _():
        at = pl.multiple_of(s * rows, rows)
        lt[:, pl.ds(at, rows), :] = to_major(left[...])
        rt[:, pl.ds(pl.multiple_of(core * half + at, rows), rows), :] = to_major(own[...])
        rt[:, pl.ds(pl.multiple_of((1 - core) * half + at, rows), rows), :] = to_major(other[...])

    @pl.when(s == steps)
    def _():
        def multiply(c, _):
            xt[c] = dot(lt[c], rt[c], 1, 1).astype(LOW)
            return 0
        lax.fori_loop(0, chan, multiply, 0, unroll=unroll)

    @pl.when(s >= steps)
    def _():
        x = to_minor(xt[:, pl.ds(pl.multiple_of((s - steps) * rows, rows), rows), :])
        for q in range(nparts):
            for c in range(2):
                start = c * half + q * nrow
                out[q, :, c * nrow:(c + 1) * nrow] = x[:, start:start + nrow]


def phases(ni, rows):
    steps = ni // rows
    inward = lambda s: jnp.minimum(s, steps - 1)
    outward = lambda s: jnp.maximum(s - steps, 0)
    return steps, inward, outward


def product_call(scal, left, own, other, nparts):
    ni, nk, chan = left.shape
    nrow = ni // nparts
    nj = 2 * ni
    rows = pick_rows(nrow)
    steps, inward, outward = phases(ni, rows)
    edge = pl.BlockSpec((rows, nk, chan), lambda s, sc: (inward(s), 0, 0))
    return pl.pallas_call(
        lambda *refs: product_kernel(nparts, 4, *refs),
        grid_spec=pltpu.PrefetchScalarGridSpec(
            num_scalar_prefetch=1,
            grid=(2 * steps,),
            in_specs=[edge] * 3,
            out_specs=pl.BlockSpec((nparts, rows, 2 * nrow, chan),
                                   lambda s, sc: (0, outward(s), 0, 0)),
            scratch_shapes=[pltpu.VMEM((chan, ni, nk), LOW), pltpu.VMEM((chan, nj, nk), LOW),
                            pltpu.VMEM((chan, ni, nj), LOW)],
        ),
        out_shape=sds((nparts, ni, 2 * nrow, chan), LOW),
        compiler_params=params(56),
        cost_estimate=cost(33),
        name="product",
    )(scal, left, own, other)


def middle_kernel(sub, z_ref, g_ref, x_ref, norms, gate_w, out_w, new, gx, gate_grad, wout, nout,
                  ylow, glow):
    rows, nk, chan = z_ref.shape

    @pl.when(pl.program_id(0) == 0)
    def _():
        wout[...] = jnp.zeros_like(wout)
        nout[...] = jnp.zeros_like(nout)

    def step(t, _):
        rng = pl.ds(t * sub, sub)
        flat = pl.ds(pl.multiple_of(t * sub * nk, sub * nk), sub * nk)
        z = z_ref[rng].astype(F32).reshape(-1, chan)
        zhat, _ = normalize(z)
        u = (zhat * norms[0:1] + norms[1:2]).astype(LOW)
        gate = sigmoid(dot(u, gate_w[...]))
        hat, inverse = normalize(x_ref[rng].astype(F32).reshape(-1, chan))
        y = (hat * norms[2:3] + norms[3:4]).astype(LOW)
        out = dot(y, out_w[...])
        so = gate * out
        new[rng] = (z + so).astype(LOW).reshape(sub, nk, chan)
        g = g_ref[rng].astype(F32).reshape(-1, chan)
        go = (g * gate).astype(LOW)
        gate_grad[rng] = (g * so * (1.0 - gate)).astype(LOW).reshape(sub, nk, chan)
        ylow[flat] = y
        glow[flat] = go
        gy = dot(go, out_w[...], 1, 1)
        nout[0] += eights(gy * hat)
        nout[1] += eights(gy)
        gx[rng] = norm_back(gy * norms[2:3], hat, inverse).astype(LOW).reshape(sub, nk, chan)
        return 0

    lax.fori_loop(0, rows // sub, step, 0)
    wout[...] += dot(ylow[...], glow[...], 0, 0)


def middle_call(z, g, x, norms, gate_w, out_w):
    ni, nk, chan = z.shape
    rows = 16
    flat = pl.BlockSpec((rows, nk, chan), lambda s: (s, 0, 0))
    low = pltpu.VMEM((rows * nk, chan), LOW)
    sums = [sds((chan, chan), F32), sds((2, 8, chan), F32)]
    return pl.pallas_call(
        lambda *refs: middle_kernel(4, *refs),
        grid=(ni // rows,),
        in_specs=[flat] * 3 + [whole_spec(v) for v in (norms, gate_w, out_w)],
        out_specs=[flat] * 3 + [whole_spec(v) for v in sums],
        out_shape=[sds(z.shape, LOW)] * 3 + sums,
        scratch_shapes=[low, low],
        compiler_params=params(40),
        cost_estimate=cost(40),
        name="middle",
    )(z, g, x, norms, gate_w, out_w)


def edge_grad_kernel(nparts, unroll, sc, left, own, other, gx, gleft, keep, send, lt, rt, gt):
    s = pl.program_id(0)
    steps = pl.num_programs(0) // 2
    rows, nk, chan = left.shape
    nrow = gx.shape[2] // 2
    half = nparts * nrow
    core = sc[0]

    @pl.when(s < steps)
    def _():
        at = pl.multiple_of(s * rows, rows)
        lt[:, pl.ds(at, rows), :] = to_major(left[...])
        rt[:, pl.ds(pl.multiple_of(core * half + at, rows), rows), :] = to_major(own[...])
        rt[:, pl.ds(pl.multiple_of((1 - core) * half + at, rows), rows), :] = to_major(other[...])
        g = jnp.concatenate([
            gx[q, :, c * nrow:(c + 1) * nrow] for c in range(2) for q in range(nparts)
        ], axis=1)
        gt[:, pl.ds(at, rows), :] = to_major(g)

    @pl.when(s == steps)
    def _():
        def multiply(c, _):
            lc, rc, gc = lt[c], rt[c], gt[c]
            lt[c] = dot(gc, rc, 1, 0).astype(LOW)
            rt[c] = dot(gc, lc, 0, 0).astype(LOW)
            return 0
        lax.fori_loop(0, chan, multiply, 0, unroll=unroll)

    @pl.when(s >= steps)
    def _():
        at = pl.multiple_of((s - steps) * rows, rows)
        gleft[...] = to_minor(lt[:, pl.ds(at, rows), :])
        keep[...] = to_minor(rt[:, pl.ds(pl.multiple_of(core * half + at, rows), rows), :])
        send[...] = to_minor(rt[:, pl.ds(pl.multiple_of((1 - core) * half + at, rows), rows), :])


def edge_grad_call(scal, left, own, other, gx):
    nparts = gx.shape[0]
    ni, nk, chan = left.shape
    nrow = ni // nparts
    nj = 2 * ni
    rows = pick_rows(nrow)
    steps, inward, outward = phases(ni, rows)
    edge = pl.BlockSpec((rows, nk, chan), lambda s, sc: (inward(s), 0, 0))
    back = pl.BlockSpec((rows, nk, chan), lambda s, sc: (outward(s), 0, 0))
    return pl.pallas_call(
        lambda *refs: edge_grad_kernel(nparts, 4, *refs),
        grid_spec=pltpu.PrefetchScalarGridSpec(
            num_scalar_prefetch=1,
            grid=(2 * steps,),
            in_specs=[edge] * 3 + [pl.BlockSpec((nparts, rows, 2 * nrow, chan),
                                                lambda s, sc: (0, inward(s), 0, 0))],
            out_specs=[back] * 3,
            scratch_shapes=[pltpu.VMEM((chan, ni, nk), LOW), pltpu.VMEM((chan, nj, nk), LOW),
                            pltpu.VMEM((chan, ni, nj), LOW)],
        ),
        out_shape=[sds(left.shape, LOW)] * 3,
        compiler_params=params(58),
        cost_estimate=cost(50),
        name="edge_grad",
    )(scal, left, own, other, gx)


def input_kernel(sub, z_ref, g_ref, gleft, keep, got, gate_grad, norms, proj, rowm, colm,
                 out, wproj, nin, ulow, plow):
    rows, nk, chan = z_ref.shape
    base = pl.program_id(0) * rows

    @pl.when(pl.program_id(0) == 0)
    def _():
        wproj[...] = jnp.zeros_like(wproj)
        nin[...] = jnp.zeros_like(nin)

    def step(t, _):
        at = t * sub
        rng = pl.ds(at, sub)
        flat = pl.ds(pl.multiple_of(at * nk, sub * nk), sub * nk)
        z = z_ref[rng].astype(F32).reshape(-1, chan)
        hat, inverse = normalize(z)
        u = (hat * norms[0:1] + norms[1:2]).astype(LOW)
        ulow[flat] = u
        p = dot(u, proj[:, :4 * chan])
        m = row_mask(rowm, colm, base + at, sub)
        gl = gleft[rng].astype(F32).reshape(-1, chan) * m
        gr = (keep[rng].astype(F32) + got[rng].astype(F32)).reshape(-1, chan) * m
        for n, grad in ((0, gl), (2, gr)):
            sig = sigmoid(p[:, (n + 1) * chan:(n + 2) * chan])
            first = grad * sig
            plow[flat, n * chan:(n + 1) * chan] = first.astype(LOW)
            second = first * (p[:, n * chan:(n + 1) * chan] * (1.0 - sig))
            plow[flat, (n + 1) * chan:(n + 2) * chan] = second.astype(LOW)
        plow[flat, 4 * chan:] = gate_grad[rng].reshape(-1, chan)
        gu = dot(plow[flat], proj[...], 1, 1)
        nin[0] += eights(gu * hat)
        nin[1] += eights(gu)
        g = g_ref[rng].astype(F32).reshape(-1, chan)
        grad_z = g + norm_back(gu * norms[0:1], hat, inverse)
        out[rng] = grad_z.astype(LOW).reshape(sub, nk, chan)
        return 0

    lax.fori_loop(0, rows // sub, step, 0)
    wproj[...] += dot(ulow[...], plow[...], 0, 0)


def input_call(z, g, gleft, keep, got, gate_grad, norms, proj, rowm, colm):
    ni, nk, chan = z.shape
    rows = 16
    flat = pl.BlockSpec((rows, nk, chan), lambda s: (s, 0, 0))
    width = proj.shape[1]
    sums = [sds((chan, width), F32), sds((2, 8, chan), F32)]
    return pl.pallas_call(
        lambda *refs: input_kernel(4, *refs),
        grid=(ni // rows,),
        in_specs=[flat] * 6 + [whole_spec(v) for v in (norms, proj, rowm, colm)],
        out_specs=[flat] + [whole_spec(v) for v in sums],
        out_shape=[sds(z.shape, LOW)] + sums,
        scratch_shapes=[pltpu.VMEM((rows * nk, chan), LOW), pltpu.VMEM((rows * nk, width), LOW)],
        compiler_params=params(40),
        cost_estimate=cost(54),
        name="input_grad",
    )(z, g, gleft, keep, got, gate_grad, norms, proj, rowm, colm)


def place_call(blocks, b, batches, whole=None):
    count, nrow, nk, chan = blocks.shape
    half = nrow // 2

    def kernel(*refs):
        refs[-1][...] = refs[0][...]

    args = [blocks] + ([] if whole is None else [whole])
    return pl.pallas_call(
        kernel,
        grid=(count, 2),
        in_specs=[pl.BlockSpec((1, half, nk, chan), lambda g, r: (g, r, 0, 0))]
        + [pl.BlockSpec(memory_space=pl.ANY)] * (len(args) - 1),
        out_specs=pl.BlockSpec((1, half, nk, chan), lambda g, r: (g * batches + b, r, 0, 0)),
        out_shape=sds((count * batches, nrow, nk, chan), LOW),
        input_output_aliases={} if whole is None else {1: 0},
        compiler_params=params(16),
        cost_estimate=cost(5),
        name="place",
    )(*args)


def shards(rows, cols, pair, cotangent, residue_mask, weights, norm_params, momentum,
           norm_momentum, average, norm_average):
    zeds = rows // 2
    crops, nrow, ncol, chan = pair.shape
    batches = crops // zeds
    length = residue_mask.shape[1]
    ni = zeds * nrow
    row = lax.axis_index("row")
    col = lax.axis_index("col")
    zed, core = row // 2, row % 2
    weight_low = weights.astype(LOW)
    project_low = jnp.concatenate([weight_low[n] for n in range(5)], axis=1)
    mask_float = residue_mask.astype(F32)
    scal = jnp.stack([core]).astype(jnp.int32)
    same_core = [[2 * q + c for q in range(zeds)] for c in range(2)]

    def zswap(blocks):
        return lax.all_to_all(blocks, "row", 0, 0, tiled=True, axis_index_groups=same_core)

    def coreswap(block):
        return lax.ppermute(block, "row", [(r, r ^ 1) for r in range(rows)])

    def after(values, *others):
        return lax.optimization_barrier((values, others))[0]

    def flat(v):
        return v.reshape(ni, ncol, chan)

    def blocked(v):
        return v.reshape(zeds, nrow, ncol, chan)

    def sum_all(term):
        count = term.shape[0] // 2
        mine = lax.dynamic_slice_in_dim(term, core * count, count, 0)
        mine = mine + coreswap(lax.dynamic_slice_in_dim(term, (1 - core) * count, count, 0))
        step = 1
        while step < cols:
            mine = mine + lax.ppermute(mine, "col", [(q, q ^ step) for q in range(cols)])
            step *= 2
        step = 2
        while step < rows:
            mine = mine + lax.ppermute(mine, "row", [(r, r ^ step) for r in range(rows)])
            step *= 2
        got = coreswap(mine)
        return jnp.concatenate([jnp.where(core == 0, mine, got), jnp.where(core == 0, got, mine)])

    masks = []
    for b in range(batches):
        crop_mask = lax.dynamic_index_in_dim(mask_float, zed * batches + b, 0, keepdims=False)
        by_block = crop_mask.reshape(zeds, 2, nrow)
        rowm = lax.dynamic_index_in_dim(by_block, core, 1, keepdims=False).reshape(-1)
        colm = lax.dynamic_slice_in_dim(crop_mask, col * ncol, ncol, 0)
        masks.append((jnp.broadcast_to(rowm[:, None], (ni, chan)),
                      jnp.broadcast_to(colm[:, None], (ncol, chan))))

    def take(whole, b):
        return whole.reshape(zeds, batches, nrow, ncol, chan)[:, b]

    def edges(b):
        left, right = edges_call(pairs[b], norm_params, project_low[:, :4 * chan], *masks[b])
        return left, right, coreswap(right)

    pairs, cots, kept, reduced = [], [], [], []
    for b in range(batches):
        block = zswap(after(take(pair, b), pairs[b - 1]) if b else take(pair, b))
        pairs.append(flat(block))
    for b in range(batches):
        block = zswap(after(take(cotangent, b), cots[b - 1] if b else pairs[-1]))
        cots.append(flat(block))
    for b in range(batches):
        if b:
            pairs[b] = after(pairs[b], part)
        kept.append(edges(b))
        part = product_call(scal, *kept[b], cols)
        if b:
            part = after(part, reduced[b - 1])
        reduced.append(flat(lax.psum_scatter(part, "col", scatter_dimension=0, tiled=True)))
    gathered, news, gates, sums = [], [], [], []
    for b in range(batches):
        new, gx, gate_grad, wout, nout = middle_call(
            pairs[b], cots[b], reduced[b], norm_params, weight_low[4], weight_low[5])
        news.append(zswap(blocked(new)))
        gx = after(gx, gathered[b - 1] if b else reduced[-1])
        gathered.append(lax.all_gather(gx, "col", axis=0))
        gates.append(gate_grad)
        sums.append((wout, nout))
    backs, flats = [], []
    for b in range(batches):
        gx = after(gathered[b], out) if b else gathered[b]
        gleft, keep, send = edge_grad_call(scal, *kept[b], gx)
        got = coreswap(send)
        out = input_call(pairs[b], cots[b], gleft, keep, got, gates[b], norm_params, project_low,
                         *masks[b])
        back, wproj, nin = out
        backs.append(zswap(blocked(back)))
        wout, nout = sums[b]
        wproj = jnp.transpose(wproj.reshape(chan, 5, chan), (1, 0, 2)).reshape(5 * chan, chan)
        flats.append(jnp.concatenate(
            [wproj, wout, jnp.sum(nin, axis=1), jnp.sum(nout, axis=1)], axis=0))

    def collect(pieces):
        whole = None
        for b in range(batches):
            whole = place_call(pieces[b], b, batches, whole)
        return whole

    new_pair = collect(news)
    pair_grad = collect(backs)
    grads = sum_all(sum(flats))
    grad_weights = grads[: 6 * chan].reshape(weights.shape)
    grad_norms = grads[6 * chan:]
    rate = 0.1 / (length * math.sqrt(crops))
    new_momentum = MOMENT * momentum + grad_weights
    new_weights = weights - rate * (grad_weights + MOMENT * new_momentum)
    new_average = DECAY * average + (1.0 - DECAY) * new_weights
    new_norm_momentum = MOMENT * norm_momentum + grad_norms
    new_norms = norm_params - rate * (grad_norms + MOMENT * new_norm_momentum)
    new_norm_average = DECAY * norm_average + (1.0 - DECAY) * new_norms
    return (new_pair, pair_grad, new_weights, new_momentum, new_average, new_norms,
            new_norm_momentum, new_norm_average)


def solution(mesh):
    rows, cols = mesh.shape["row"], mesh.shape["col"]
    tiled = P(None, "row", "col", None)

    def body(*args):
        return shards(rows, cols, *args)

    return jax.shard_map(
        body,
        mesh=mesh,
        in_specs=(tiled, tiled) + (P(),) * 7,
        out_specs=(tiled, tiled) + (P(),) * 6,
        check_vma=False,
    )
```

```python
import math

import jax
import jax.numpy as jnp
from jax import lax
from jax.experimental import pallas as pl
from jax.experimental.pallas import tpu as pltpu
from jax.sharding import PartitionSpec as P

EPS = 1e-05
MOMENT = 0.9
DECAY = 0.8
LOW = jnp.bfloat16
F32 = jnp.float32
MIB = 1 << 20
SHARE = 6_000_000_000


def sds(shape, dtype):
    return jax.ShapeDtypeStruct(shape, dtype)


def params(mib):
    return pltpu.CompilerParams(vmem_limit_bytes=mib * MIB)


def cost(micros):
    return pl.CostEstimate(flops=int(micros * SHARE), bytes_accessed=0, transcendentals=0)


def sigmoid(v):
    return 0.5 * jnp.tanh(0.5 * v) + 0.5


def normalize(v):
    center = v - jnp.mean(v, axis=-1, keepdims=True)
    inverse = lax.rsqrt(jnp.mean(center * center, axis=-1, keepdims=True) + EPS)
    return center * inverse, inverse


def norm_back(grad_hat, normed, inverse):
    first = jnp.mean(grad_hat, axis=-1, keepdims=True)
    second = jnp.mean(grad_hat * normed, axis=-1, keepdims=True)
    return inverse * (grad_hat - first - normed * second)


def dot(a, b, ca=1, cb=0):
    return lax.dot_general(a, b, (((ca,), (cb,)), ((), ())), preferred_element_type=F32)


def eights(v):
    return jnp.sum(v.reshape(-1, 8, v.shape[-1]), axis=0)


def to_major(v):
    return jnp.swapaxes(jnp.swapaxes(v, 1, 2), 0, 1)


def to_minor(v):
    return jnp.swapaxes(jnp.swapaxes(v, 0, 1), 1, 2)


def row_mask(rowm, colm, start, count):
    m = rowm[pl.ds(start, count)][:, None, :] * colm[...][None]
    return m.reshape(-1, m.shape[-1])


def pick_rows(nrow):
    return 16 if nrow % 16 == 0 else 8


def whole_spec(array):
    return pl.BlockSpec(array.shape, lambda s: (0,) * len(array.shape))


def edges_kernel(sub, z_ref, norms, proj, rowm, colm, left, right):
    rows, nk, chan = z_ref.shape
    base = pl.program_id(0) * rows

    def step(t, _):
        at = t * sub
        z = z_ref[pl.ds(at, sub)].astype(F32).reshape(-1, chan)
        hat, _ = normalize(z)
        u = (hat * norms[0:1] + norms[1:2]).astype(LOW)
        p = dot(u, proj[...])
        m = row_mask(rowm, colm, base + at, sub)
        lv = sigmoid(p[:, chan:2 * chan]) * p[:, :chan] * m
        rv = sigmoid(p[:, 3 * chan:]) * p[:, 2 * chan:3 * chan] * m
        left[pl.ds(at, sub)] = lv.astype(LOW).reshape(sub, nk, chan)
        right[pl.ds(at, sub)] = rv.astype(LOW).reshape(sub, nk, chan)
        return 0

    lax.fori_loop(0, rows // sub, step, 0)


def edges_call(z, norms, proj, rowm, colm):
    ni, nk, chan = z.shape
    rows = 16
    flat = pl.BlockSpec((rows, nk, chan), lambda s: (s, 0, 0))
    return pl.pallas_call(
        lambda *refs: edges_kernel(4, *refs),
        grid=(ni // rows,),
        in_specs=[flat] + [whole_spec(v) for v in (norms, proj, rowm, colm)],
        out_specs=[flat, flat],
        out_shape=[sds(z.shape, LOW)] * 2,
        compiler_params=params(58),
        cost_estimate=cost(27),
        name="edges",
    )(z, norms, proj, rowm, colm)


def product_kernel(nparts, unroll, sc, left, own, other, out, lt, rt, xt):
    s = pl.program_id(0)
    steps = pl.num_programs(0) // 2
    rows, nk, chan = left.shape
    nrow = out.shape[2] // 2
    half = nparts * nrow
    core = sc[0]

    @pl.when(s < steps)
    def _():
        at = pl.multiple_of(s * rows, rows)
        lt[:, pl.ds(at, rows), :] = to_major(left[...])
        rt[:, pl.ds(pl.multiple_of(core * half + at, rows), rows), :] = to_major(own[...])
        rt[:, pl.ds(pl.multiple_of((1 - core) * half + at, rows), rows), :] = to_major(other[...])

    @pl.when(s == steps)
    def _():
        def multiply(c, _):
            xt[c] = dot(lt[c], rt[c], 1, 1).astype(LOW)
            return 0
        lax.fori_loop(0, chan, multiply, 0, unroll=unroll)

    @pl.when(s >= steps)
    def _():
        x = to_minor(xt[:, pl.ds(pl.multiple_of((s - steps) * rows, rows), rows), :])
        for q in range(nparts):
            for c in range(2):
                start = c * half + q * nrow
                out[q, :, c * nrow:(c + 1) * nrow] = x[:, start:start + nrow]


def phases(ni, rows):
    steps = ni // rows
    inward = lambda s: jnp.minimum(s, steps - 1)
    outward = lambda s: jnp.maximum(s - steps, 0)
    return steps, inward, outward


def product_call(scal, left, own, other, nparts, micros):
    ni, nk, chan = left.shape
    nrow = ni // nparts
    nj = 2 * ni
    rows = pick_rows(nrow)
    steps, inward, outward = phases(ni, rows)
    edge = pl.BlockSpec((rows, nk, chan), lambda s, sc: (inward(s), 0, 0))
    return pl.pallas_call(
        lambda *refs: product_kernel(nparts, 4, *refs),
        grid_spec=pltpu.PrefetchScalarGridSpec(
            num_scalar_prefetch=1,
            grid=(2 * steps,),
            in_specs=[edge] * 3,
            out_specs=pl.BlockSpec((nparts, rows, 2 * nrow, chan),
                                   lambda s, sc: (0, outward(s), 0, 0)),
            scratch_shapes=[pltpu.VMEM((chan, ni, nk), LOW), pltpu.VMEM((chan, nj, nk), LOW),
                            pltpu.VMEM((chan, ni, nj), LOW)],
        ),
        out_shape=sds((nparts, ni, 2 * nrow, chan), LOW),
        compiler_params=params(58),
        cost_estimate=cost(micros),
        name="product",
    )(scal, left, own, other)


def middle_kernel(sub, z_ref, g_ref, x_ref, norms, gate_w, out_w, new, gx, gate_grad, wout, nout,
                  ylow, glow):
    rows, nk, chan = z_ref.shape

    @pl.when(pl.program_id(0) == 0)
    def _():
        wout[...] = jnp.zeros_like(wout)
        nout[...] = jnp.zeros_like(nout)

    def step(t, _):
        rng = pl.ds(t * sub, sub)
        flat = pl.ds(pl.multiple_of(t * sub * nk, sub * nk), sub * nk)
        z = z_ref[rng].astype(F32).reshape(-1, chan)
        zhat, _ = normalize(z)
        u = (zhat * norms[0:1] + norms[1:2]).astype(LOW)
        gate = sigmoid(dot(u, gate_w[...]))
        hat, inverse = normalize(x_ref[rng].astype(F32).reshape(-1, chan))
        y = (hat * norms[2:3] + norms[3:4]).astype(LOW)
        out = dot(y, out_w[...])
        so = gate * out
        new[rng] = (z + so).astype(LOW).reshape(sub, nk, chan)
        g = g_ref[rng].astype(F32).reshape(-1, chan)
        go = (g * gate).astype(LOW)
        gate_grad[rng] = (g * so * (1.0 - gate)).astype(LOW).reshape(sub, nk, chan)
        ylow[flat] = y
        glow[flat] = go
        gy = dot(go, out_w[...], 1, 1)
        nout[0] += eights(gy * hat)
        nout[1] += eights(gy)
        gx[rng] = norm_back(gy * norms[2:3], hat, inverse).astype(LOW).reshape(sub, nk, chan)
        return 0

    lax.fori_loop(0, rows // sub, step, 0)
    wout[...] += dot(ylow[...], glow[...], 0, 0)


def middle_call(z, g, x, norms, gate_w, out_w):
    ni, nk, chan = z.shape
    rows = 16
    flat = pl.BlockSpec((rows, nk, chan), lambda s: (s, 0, 0))
    low = pltpu.VMEM((rows * nk, chan), LOW)
    sums = [sds((chan, chan), F32), sds((2, 8, chan), F32)]
    return pl.pallas_call(
        lambda *refs: middle_kernel(4, *refs),
        grid=(ni // rows,),
        in_specs=[flat] * 3 + [whole_spec(v) for v in (norms, gate_w, out_w)],
        out_specs=[flat] * 3 + [whole_spec(v) for v in sums],
        out_shape=[sds(z.shape, LOW)] * 3 + sums,
        scratch_shapes=[low, low],
        compiler_params=params(58),
        cost_estimate=cost(40),
        name="middle",
    )(z, g, x, norms, gate_w, out_w)


def edge_grad_kernel(nparts, unroll, sc, left, own, other, gx, gleft, keep, send, lt, rt, gt):
    s = pl.program_id(0)
    steps = pl.num_programs(0) // 2
    rows, nk, chan = left.shape
    nrow = gx.shape[2] // 2
    half = nparts * nrow
    core = sc[0]

    @pl.when(s < steps)
    def _():
        at = pl.multiple_of(s * rows, rows)
        lt[:, pl.ds(at, rows), :] = to_major(left[...])
        rt[:, pl.ds(pl.multiple_of(core * half + at, rows), rows), :] = to_major(own[...])
        rt[:, pl.ds(pl.multiple_of((1 - core) * half + at, rows), rows), :] = to_major(other[...])
        g = jnp.concatenate([
            gx[q, :, c * nrow:(c + 1) * nrow] for c in range(2) for q in range(nparts)
        ], axis=1)
        gt[:, pl.ds(at, rows), :] = to_major(g)

    @pl.when(s == steps)
    def _():
        def multiply(c, _):
            lc, rc, gc = lt[c], rt[c], gt[c]
            lt[c] = dot(gc, rc, 1, 0).astype(LOW)
            rt[c] = dot(gc, lc, 0, 0).astype(LOW)
            return 0
        lax.fori_loop(0, chan, multiply, 0, unroll=unroll)

    @pl.when(s >= steps)
    def _():
        at = pl.multiple_of((s - steps) * rows, rows)
        gleft[...] = to_minor(lt[:, pl.ds(at, rows), :])
        keep[...] = to_minor(rt[:, pl.ds(pl.multiple_of(core * half + at, rows), rows), :])
        send[...] = to_minor(rt[:, pl.ds(pl.multiple_of((1 - core) * half + at, rows), rows), :])


def edge_grad_call(scal, left, own, other, gx, token):
    tokens = [] if token is None else [token]
    nparts = gx.shape[0]
    ni, nk, chan = left.shape
    nrow = ni // nparts
    nj = 2 * ni
    rows = pick_rows(nrow)
    steps, inward, outward = phases(ni, rows)
    edge = pl.BlockSpec((rows, nk, chan), lambda s, sc: (inward(s), 0, 0))
    back = pl.BlockSpec((rows, nk, chan), lambda s, sc: (outward(s), 0, 0))
    return pl.pallas_call(
        lambda *refs: edge_grad_kernel(nparts, 4, *refs[:5], *refs[5 + len(tokens):]),
        grid_spec=pltpu.PrefetchScalarGridSpec(
            num_scalar_prefetch=1,
            grid=(2 * steps,),
            in_specs=[edge] * 3 + [pl.BlockSpec((nparts, rows, 2 * nrow, chan),
                                                lambda s, sc: (0, inward(s), 0, 0))]
            + [pl.BlockSpec(memory_space=pl.ANY)] * len(tokens),
            out_specs=[back] * 3,
            scratch_shapes=[pltpu.VMEM((chan, ni, nk), LOW), pltpu.VMEM((chan, nj, nk), LOW),
                            pltpu.VMEM((chan, ni, nj), LOW)],
        ),
        out_shape=[sds(left.shape, LOW)] * 3,
        compiler_params=params(58),
        cost_estimate=cost(5),
        name="edge_grad",
    )(scal, left, own, other, gx, *tokens)


def input_kernel(sub, z_ref, g_ref, gleft, keep, got, gate_grad, norms, proj, rowm, colm,
                 out, wproj, nin, ulow, plow):
    rows, nk, chan = z_ref.shape

    @pl.when((pl.program_id(0) == 0) & (pl.program_id(1) == 0))
    def _():
        wproj[...] = jnp.zeros_like(wproj)
        nin[...] = jnp.zeros_like(nin)

    def step(t, _):
        at = t * sub
        rng = pl.ds(at, sub)
        flat = pl.ds(pl.multiple_of(at * nk, sub * nk), sub * nk)
        z = z_ref[rng].astype(F32).reshape(-1, chan)
        hat, inverse = normalize(z)
        u = (hat * norms[0:1] + norms[1:2]).astype(LOW)
        ulow[flat] = u
        p = dot(u, proj[:, :4 * chan])
        m = row_mask(rowm.at[0], colm, at, sub)
        gl = gleft[rng].astype(F32).reshape(-1, chan) * m
        gr = (keep[rng].astype(F32) + got[rng].astype(F32)).reshape(-1, chan) * m
        for n, grad in ((0, gl), (2, gr)):
            sig = sigmoid(p[:, (n + 1) * chan:(n + 2) * chan])
            first = grad * sig
            plow[flat, n * chan:(n + 1) * chan] = first.astype(LOW)
            second = first * (p[:, n * chan:(n + 1) * chan] * (1.0 - sig))
            plow[flat, (n + 1) * chan:(n + 2) * chan] = second.astype(LOW)
        plow[flat, 4 * chan:] = gate_grad[rng].reshape(-1, chan)
        gu = dot(plow[flat], proj[...], 1, 1)
        nin[0] += eights(gu * hat)
        nin[1] += eights(gu)
        g = g_ref[rng].astype(F32).reshape(-1, chan)
        grad_z = g + norm_back(gu * norms[0:1], hat, inverse)
        out[rng] = grad_z.astype(LOW).reshape(sub, nk, chan)
        return 0

    lax.fori_loop(0, rows // sub, step, 0)
    wproj[...] += dot(ulow[...], plow[...], 0, 0)


def input_call(z, g, gleft, keep, got, gate_grad, norms, proj, rowm, colm, nblocks, h, parts,
               micros):
    ni, nk, chan = z.shape
    nrow = ni // nblocks
    rows = nrow // 4
    sub = 4 if rows % 4 == 0 else 2
    per = 4 // parts
    flat = pl.BlockSpec((rows, nk, chan), lambda s, r: (s * 4 + h * per + r, 0, 0))
    mask = pl.BlockSpec((1, rows, chan), lambda s, r: (s * 4 + h * per + r, 0, 0))
    rowm = rowm.reshape(-1, rows, chan)
    width = proj.shape[1]
    sums = [sds((chan, width), F32), sds((2, 8, chan), F32)]
    whole = lambda v: pl.BlockSpec(v.shape, lambda s, r: (0,) * len(v.shape))
    return pl.pallas_call(
        lambda *refs: input_kernel(sub, *refs),
        grid=(nblocks, per),
        in_specs=[flat] * 6 + [whole(norms), whole(proj), mask, whole(colm)],
        out_specs=[pl.BlockSpec((rows, nk, chan), lambda s, r: (s * per + r, 0, 0))]
        + [whole(v) for v in sums],
        out_shape=[sds((ni // parts, nk, chan), LOW)] + sums,
        scratch_shapes=[pltpu.VMEM((rows * nk, chan), LOW), pltpu.VMEM((rows * nk, width), LOW)],
        compiler_params=params(58),
        cost_estimate=cost(micros),
        name="input_grad",
    )(z, g, gleft, keep, got, gate_grad, norms, proj, rowm, colm)


def place_call(blocks, b, batches, h, parts, whole=None):
    count, size, nk, chan = blocks.shape

    def kernel(*refs):
        refs[-2][...] = refs[0][...]
        refs[-1][...] = jnp.zeros_like(refs[-1])

    args = [blocks] + ([] if whole is None else [whole])
    return pl.pallas_call(
        kernel,
        grid=(count, 2),
        in_specs=[pl.BlockSpec((1, size // 2, nk, chan), lambda g, r: (g, r, 0, 0))]
        + [pl.BlockSpec(memory_space=pl.ANY)] * (len(args) - 1),
        out_specs=[pl.BlockSpec((1, size // 2, nk, chan),
                                lambda g, r: (g * batches + b, h * 2 + r, 0, 0)),
                   pl.BlockSpec((8, 128), lambda g, r: (0, 0))],
        out_shape=[sds((count * batches, size * parts, nk, chan), LOW), sds((8, 128), F32)],
        input_output_aliases={} if whole is None else {1: 0},
        compiler_params=params(58),
        cost_estimate=cost(0.02),
        name="place",
    )(*args)


def shards(rows, cols, pair, cotangent, residue_mask, weights, norm_params, momentum,
           norm_momentum, average, norm_average):
    zeds = rows // 2
    crops, nrow, ncol, chan = pair.shape
    batches = crops // zeds
    length = residue_mask.shape[1]
    ni = zeds * nrow
    row = lax.axis_index("row")
    col = lax.axis_index("col")
    zed, core = row // 2, row % 2
    weight_low = weights.astype(LOW)
    project_low = jnp.concatenate([weight_low[n] for n in range(5)], axis=1)
    mask_float = residue_mask.astype(F32)
    scal = jnp.stack([core]).astype(jnp.int32)
    same_core = [[2 * q + c for q in range(zeds)] for c in range(2)]

    def zswap(blocks):
        return lax.all_to_all(blocks, "row", 0, 0, tiled=True, axis_index_groups=same_core)

    def coreswap(block):
        return lax.ppermute(block, "row", [(r, r ^ 1) for r in range(rows)])

    def after(values, *others):
        return lax.optimization_barrier((values, others))[0]

    def flat(v):
        return v.reshape(ni, ncol, chan)

    def blocked(v):
        return v.reshape(zeds, nrow, ncol, chan)

    def sum_all(term, first, second):
        count = term.shape[0] // 2
        mine = lax.dynamic_slice_in_dim(term, core * count, count, 0)
        mine = mine + coreswap(lax.dynamic_slice_in_dim(term, (1 - core) * count, count, 0))
        step = 1
        while step < cols:
            mine = mine + lax.ppermute(mine, "col", [(q, q ^ step) for q in range(cols)])
            step *= 2
        mine = after(mine, first)
        step = 2
        while step < rows:
            if step * 2 >= rows:
                mine = mine + second[:1]
            mine = mine + lax.ppermute(mine, "row", [(r, r ^ step) for r in range(rows)])
            step *= 2
        got = coreswap(mine)
        return jnp.concatenate([jnp.where(core == 0, mine, got), jnp.where(core == 0, got, mine)])

    masks = []
    for b in range(batches):
        crop_mask = lax.dynamic_index_in_dim(mask_float, zed * batches + b, 0, keepdims=False)
        by_block = crop_mask.reshape(zeds, 2, nrow)
        rowm = lax.dynamic_index_in_dim(by_block, core, 1, keepdims=False).reshape(-1)
        colm = lax.dynamic_slice_in_dim(crop_mask, col * ncol, ncol, 0)
        masks.append((jnp.broadcast_to(rowm[:, None], (ni, chan)),
                      jnp.broadcast_to(colm[:, None], (ncol, chan))))

    def take(whole, b):
        return whole.reshape(zeds, batches, nrow, ncol, chan)[:, b]

    def edges(b):
        left, right = edges_call(pairs[b], norm_params, project_low[:, :4 * chan], *masks[b])
        return left, right, coreswap(right)

    pairs, cots, kept, reduced = [], [], [], []
    last = None
    for b in range(batches):
        block = take(after(pair, block), b) if b else take(pair, b)
        last = zswap(after(block, last) if b else block)
        pairs.append(flat(last))
    for b in range(batches):
        last = zswap(take(after(cotangent, last), b))
        cots.append(flat(last))
    for b in range(batches):
        if b:
            pairs[b] = after(pairs[b], part)
        left, right, other = edges(b)
        kept.append((left, right, other))
        part = product_call(scal, left, right, other, cols, 33 if b else 3)
        ready = after(part, reduced[b - 1], cots[b - 1]) if b else part
        reduced.append(flat(lax.psum_scatter(ready, "col", scatter_dimension=0, tiled=True)))
    def collect(pieces, whole=None):
        token = None
        for blocks, b, h, share in pieces:
            whole, token = place_call(blocks, b, batches, h, share, whole)
        return whole, token

    gathered, news, gates, sums = [], [], [], []
    for b in range(batches):
        new, gx, gate_grad, wout, nout = middle_call(
            pairs[b], cots[b], reduced[b], norm_params, weight_low[4], weight_low[5])
        last = zswap(after(blocked(new), last))
        news.append((last, b, 0, 1))
        ready = after(gx, (gathered[b - 1], last) if b else reduced[-1])
        gathered.append(lax.all_gather(ready, "col", axis=0))
        gates.append(gate_grad)
        sums.append((wout, nout))
    new_pair, placed = collect(news)
    backs, flats = [], []
    for b in range(batches):
        grad = after(gathered[b], out) if b else gathered[b]
        gleft, keep, send = edge_grad_call(scal, *kept[b], grad, placed if b else None)
        got = coreswap(send)
        if b:
            got = after(got, last)
        share = 2 if b == batches - 1 else 1
        for h in range(share):
            out = input_call(pairs[b], cots[b], gleft, keep, got, gates[b], norm_params,
                             project_low, *masks[b], zeds, h, share, 27 if b == batches - 1 else 5)
            back, wproj, nin = out
            last = zswap(after(back.reshape(zeds, nrow // share, ncol, chan), last))
            backs.append((last, b, h, share))
            grads = (wproj, nin) if h == 0 else (grads[0] + wproj, grads[1] + nin)
        wproj, nin = grads
        wout, nout = sums[b]
        wproj = jnp.transpose(wproj.reshape(chan, 5, chan), (1, 0, 2)).reshape(5 * chan, chan)
        flats.append(jnp.concatenate(
            [wproj, wout, jnp.sum(nin, axis=1), jnp.sum(nout, axis=1)], axis=0))

    pair_grad, first = collect(backs[:-2]) if batches > 1 else (None, None)
    pair_grad, second = collect(backs[-2:-1], pair_grad)
    pair_grad, _ = collect(backs[-1:], pair_grad)
    term = sum(flats) if first is None else sum(flats) + first[:1]
    grads = sum_all(term, backs[-2][0], second)
    grad_weights = grads[: 6 * chan].reshape(weights.shape)
    grad_norms = grads[6 * chan:]
    rate = 0.1 / (length * math.sqrt(crops))
    new_momentum = MOMENT * momentum + grad_weights
    new_weights = weights - rate * (grad_weights + MOMENT * new_momentum)
    new_average = DECAY * average + (1.0 - DECAY) * new_weights
    new_norm_momentum = MOMENT * norm_momentum + grad_norms
    new_norms = norm_params - rate * (grad_norms + MOMENT * new_norm_momentum)
    new_norm_average = DECAY * norm_average + (1.0 - DECAY) * new_norms
    return (new_pair, pair_grad, new_weights, new_momentum, new_average, new_norms,
            new_norm_momentum, new_norm_average)


def solution(mesh):
    rows, cols = mesh.shape["row"], mesh.shape["col"]
    tiled = P(None, "row", "col", None)

    def body(*args):
        return shards(rows, cols, *args)

    return jax.shard_map(
        body,
        mesh=mesh,
        in_specs=(tiled, tiled) + (P(),) * 7,
        out_specs=(tiled, tiled) + (P(),) * 6,
        check_vma=False,
    )
```

```python
import math

import jax
import jax.numpy as jnp
from jax import lax
from jax.experimental import pallas as pl
from jax.experimental.pallas import tpu as pltpu
from jax.sharding import PartitionSpec as P

EPS = 1e-05
MOMENT = 0.9
DECAY = 0.8
LOW = jnp.bfloat16
F32 = jnp.float32
MIB = 1 << 20
SHARE = 6_000_000_000


def sds(shape, dtype):
    return jax.ShapeDtypeStruct(shape, dtype)


def params(mib):
    return pltpu.CompilerParams(vmem_limit_bytes=mib * MIB)


def cost(micros):
    return pl.CostEstimate(flops=int(micros * SHARE), bytes_accessed=0, transcendentals=0)


def sigmoid(v):
    return 0.5 * jnp.tanh(0.5 * v) + 0.5


def normalize(v):
    center = v - jnp.mean(v, axis=-1, keepdims=True)
    inverse = lax.rsqrt(jnp.mean(center * center, axis=-1, keepdims=True) + EPS)
    return center * inverse, inverse


def norm_back(grad_hat, normed, inverse):
    first = jnp.mean(grad_hat, axis=-1, keepdims=True)
    second = jnp.mean(grad_hat * normed, axis=-1, keepdims=True)
    return inverse * (grad_hat - first - normed * second)


def dot(a, b, ca=1, cb=0):
    return lax.dot_general(a, b, (((ca,), (cb,)), ((), ())), preferred_element_type=F32)


def eights(v):
    return jnp.sum(v.reshape(-1, 8, v.shape[-1]), axis=0)


def to_major(v):
    return jnp.swapaxes(jnp.swapaxes(v, 1, 2), 0, 1)


def to_minor(v):
    return jnp.swapaxes(jnp.swapaxes(v, 0, 1), 1, 2)


def row_mask(rowm, colm, start, count):
    m = rowm[pl.ds(start, count)][:, None, :] * colm[...][None]
    return m.reshape(-1, m.shape[-1])


def pick_rows(nrow):
    return 16 if nrow % 16 == 0 else 8


def whole_spec(array):
    return pl.BlockSpec(array.shape, lambda s: (0,) * len(array.shape))


def edges_kernel(sub, z_ref, norms, proj, rowm, colm, left, right):
    rows, nk, chan = z_ref.shape
    base = pl.program_id(0) * rows

    def step(t, _):
        at = t * sub
        z = z_ref[pl.ds(at, sub)].astype(F32).reshape(-1, chan)
        hat, _ = normalize(z)
        u = (hat * norms[0:1] + norms[1:2]).astype(LOW)
        p = dot(u, proj[...])
        m = row_mask(rowm, colm, base + at, sub)
        lv = sigmoid(p[:, chan:2 * chan]) * p[:, :chan] * m
        rv = sigmoid(p[:, 3 * chan:]) * p[:, 2 * chan:3 * chan] * m
        left[pl.ds(at, sub)] = lv.astype(LOW).reshape(sub, nk, chan)
        right[pl.ds(at, sub)] = rv.astype(LOW).reshape(sub, nk, chan)
        return 0

    lax.fori_loop(0, rows // sub, step, 0, unroll=rows // sub)


def edges_call(z, norms, proj, rowm, colm):
    ni, nk, chan = z.shape
    rows = 32
    flat = pl.BlockSpec((rows, nk, chan), lambda s: (s, 0, 0))
    return pl.pallas_call(
        lambda *refs: edges_kernel(8, *refs),
        grid=(ni // rows,),
        in_specs=[flat] + [whole_spec(v) for v in (norms, proj, rowm, colm)],
        out_specs=[flat, flat],
        out_shape=[sds(z.shape, LOW)] * 2,
        compiler_params=params(58),
        cost_estimate=cost(27),
        name="edges",
    )(z, norms, proj, rowm, colm)


def product_kernel(nparts, unroll, sc, left, own, other, out, lt, rt, xt):
    s = pl.program_id(0)
    steps = pl.num_programs(0) // 2
    rows, nk, chan = left.shape
    nrow = out.shape[2] // 2
    half = nparts * nrow
    core = sc[0]

    @pl.when(s < steps)
    def _():
        at = pl.multiple_of(s * rows, rows)
        lt[:, pl.ds(at, rows), :] = to_major(left[...])
        rt[:, pl.ds(pl.multiple_of(core * half + at, rows), rows), :] = to_major(own[...])
        rt[:, pl.ds(pl.multiple_of((1 - core) * half + at, rows), rows), :] = to_major(other[...])

    @pl.when(s == steps)
    def _():
        def multiply(c, _):
            xt[c] = dot(lt[c], rt[c], 1, 1).astype(LOW)
            return 0
        lax.fori_loop(0, chan, multiply, 0, unroll=unroll)

    @pl.when(s >= steps)
    def _():
        x = to_minor(xt[:, pl.ds(pl.multiple_of((s - steps) * rows, rows), rows), :])
        for q in range(nparts):
            for c in range(2):
                start = c * half + q * nrow
                out[q, :, c * nrow:(c + 1) * nrow] = x[:, start:start + nrow]


def phases(ni, rows):
    steps = ni // rows
    inward = lambda s: jnp.minimum(s, steps - 1)
    outward = lambda s: jnp.maximum(s - steps, 0)
    return steps, inward, outward


def product_call(scal, left, own, other, nparts, micros):
    ni, nk, chan = left.shape
    nrow = ni // nparts
    nj = 2 * ni
    rows = pick_rows(nrow)
    steps, inward, outward = phases(ni, rows)
    edge = pl.BlockSpec((rows, nk, chan), lambda s, sc: (inward(s), 0, 0))
    return pl.pallas_call(
        lambda *refs: product_kernel(nparts, 16, *refs),
        grid_spec=pltpu.PrefetchScalarGridSpec(
            num_scalar_prefetch=1,
            grid=(2 * steps,),
            in_specs=[edge] * 3,
            out_specs=pl.BlockSpec((nparts, rows, 2 * nrow, chan),
                                   lambda s, sc: (0, outward(s), 0, 0)),
            scratch_shapes=[pltpu.VMEM((chan, ni, nk), LOW), pltpu.VMEM((chan, nj, nk), LOW),
                            pltpu.VMEM((chan, ni, nj), LOW)],
        ),
        out_shape=sds((nparts, ni, 2 * nrow, chan), LOW),
        compiler_params=params(58),
        cost_estimate=cost(micros),
        name="product",
    )(scal, left, own, other)


def middle_kernel(sub, z_ref, g_ref, x_ref, norms, gate_w, out_w, new, gx, gate_grad, wout, nout,
                  ylow, glow):
    rows, nk, chan = z_ref.shape

    @pl.when(pl.program_id(0) == 0)
    def _():
        wout[...] = jnp.zeros_like(wout)
        nout[...] = jnp.zeros_like(nout)

    def step(t, _):
        rng = pl.ds(t * sub, sub)
        flat = pl.ds(pl.multiple_of(t * sub * nk, sub * nk), sub * nk)
        z = z_ref[rng].astype(F32).reshape(-1, chan)
        zhat, _ = normalize(z)
        u = (zhat * norms[0:1] + norms[1:2]).astype(LOW)
        gate = sigmoid(dot(u, gate_w[...]))
        hat, inverse = normalize(x_ref[rng].astype(F32).reshape(-1, chan))
        y = (hat * norms[2:3] + norms[3:4]).astype(LOW)
        out = dot(y, out_w[...])
        so = gate * out
        new[rng] = (z + so).astype(LOW).reshape(sub, nk, chan)
        g = g_ref[rng].astype(F32).reshape(-1, chan)
        go = (g * gate).astype(LOW)
        gate_grad[rng] = (g * so * (1.0 - gate)).astype(LOW).reshape(sub, nk, chan)
        ylow[flat] = y
        glow[flat] = go
        gy = dot(go, out_w[...], 1, 1)
        nout[0] += eights(gy * hat)
        nout[1] += eights(gy)
        gx[rng] = norm_back(gy * norms[2:3], hat, inverse).astype(LOW).reshape(sub, nk, chan)
        return 0

    lax.fori_loop(0, rows // sub, step, 0, unroll=rows // sub)
    wout[...] += dot(ylow[...], glow[...], 0, 0)


def middle_call(z, g, x, norms, gate_w, out_w):
    ni, nk, chan = z.shape
    rows = 16
    flat = pl.BlockSpec((rows, nk, chan), lambda s: (s, 0, 0))
    low = pltpu.VMEM((rows * nk, chan), LOW)
    sums = [sds((chan, chan), F32), sds((2, 8, chan), F32)]
    return pl.pallas_call(
        lambda *refs: middle_kernel(8, *refs),
        grid=(ni // rows,),
        in_specs=[flat] * 3 + [whole_spec(v) for v in (norms, gate_w, out_w)],
        out_specs=[flat] * 3 + [whole_spec(v) for v in sums],
        out_shape=[sds(z.shape, LOW)] * 3 + sums,
        scratch_shapes=[low, low],
        compiler_params=params(58),
        cost_estimate=cost(40),
        name="middle",
    )(z, g, x, norms, gate_w, out_w)


def edge_grad_kernel(nparts, unroll, sc, left, own, other, gx, gleft, keep, send, lt, rt, gt):
    s = pl.program_id(0)
    steps = pl.num_programs(0) // 2
    rows, nk, chan = left.shape
    nrow = gx.shape[2] // 2
    half = nparts * nrow
    core = sc[0]

    @pl.when(s < steps)
    def _():
        at = pl.multiple_of(s * rows, rows)
        lt[:, pl.ds(at, rows), :] = to_major(left[...])
        rt[:, pl.ds(pl.multiple_of(core * half + at, rows), rows), :] = to_major(own[...])
        rt[:, pl.ds(pl.multiple_of((1 - core) * half + at, rows), rows), :] = to_major(other[...])
        g = jnp.concatenate([
            gx[q, :, c * nrow:(c + 1) * nrow] for c in range(2) for q in range(nparts)
        ], axis=1)
        gt[:, pl.ds(at, rows), :] = to_major(g)

    @pl.when(s == steps)
    def _():
        def multiply(c, _):
            lc, rc, gc = lt[c], rt[c], gt[c]
            lt[c] = dot(gc, rc, 1, 0).astype(LOW)
            rt[c] = dot(gc, lc, 0, 0).astype(LOW)
            return 0
        lax.fori_loop(0, chan, multiply, 0, unroll=unroll)

    @pl.when(s >= steps)
    def _():
        at = pl.multiple_of((s - steps) * rows, rows)
        gleft[...] = to_minor(lt[:, pl.ds(at, rows), :])
        keep[...] = to_minor(rt[:, pl.ds(pl.multiple_of(core * half + at, rows), rows), :])
        send[...] = to_minor(rt[:, pl.ds(pl.multiple_of((1 - core) * half + at, rows), rows), :])


def edge_grad_call(scal, left, own, other, gx, token):
    tokens = [] if token is None else [token]
    nparts = gx.shape[0]
    ni, nk, chan = left.shape
    nrow = ni // nparts
    nj = 2 * ni
    rows = pick_rows(nrow)
    steps, inward, outward = phases(ni, rows)
    edge = pl.BlockSpec((rows, nk, chan), lambda s, sc: (inward(s), 0, 0))
    back = pl.BlockSpec((rows, nk, chan), lambda s, sc: (outward(s), 0, 0))
    return pl.pallas_call(
        lambda *refs: edge_grad_kernel(nparts, 16, *refs[:5], *refs[5 + len(tokens):]),
        grid_spec=pltpu.PrefetchScalarGridSpec(
            num_scalar_prefetch=1,
            grid=(2 * steps,),
            in_specs=[edge] * 3 + [pl.BlockSpec((nparts, rows, 2 * nrow, chan),
                                                lambda s, sc: (0, inward(s), 0, 0))]
            + [pl.BlockSpec(memory_space=pl.ANY)] * len(tokens),
            out_specs=[back] * 3,
            scratch_shapes=[pltpu.VMEM((chan, ni, nk), LOW), pltpu.VMEM((chan, nj, nk), LOW),
                            pltpu.VMEM((chan, ni, nj), LOW)],
        ),
        out_shape=[sds(left.shape, LOW)] * 3,
        compiler_params=params(58),
        cost_estimate=cost(5),
        name="edge_grad",
    )(scal, left, own, other, gx, *tokens)


def input_kernel(sub, z_ref, g_ref, gleft, keep, got, gate_grad, norms, proj, rowm, colm,
                 out, wproj, nin, ulow, plow):
    rows, nk, chan = z_ref.shape

    @pl.when((pl.program_id(0) == 0) & (pl.program_id(1) == 0))
    def _():
        wproj[...] = jnp.zeros_like(wproj)
        nin[...] = jnp.zeros_like(nin)

    def step(t, _):
        at = t * sub
        rng = pl.ds(at, sub)
        flat = pl.ds(pl.multiple_of(at * nk, sub * nk), sub * nk)
        z = z_ref[rng].astype(F32).reshape(-1, chan)
        hat, inverse = normalize(z)
        u = (hat * norms[0:1] + norms[1:2]).astype(LOW)
        ulow[flat] = u
        p = dot(u, proj[:, :4 * chan])
        m = row_mask(rowm.at[0], colm, at, sub)
        gl = gleft[rng].astype(F32).reshape(-1, chan) * m
        gr = (keep[rng].astype(F32) + got[rng].astype(F32)).reshape(-1, chan) * m
        for n, grad in ((0, gl), (2, gr)):
            sig = sigmoid(p[:, (n + 1) * chan:(n + 2) * chan])
            first = grad * sig
            plow[flat, n * chan:(n + 1) * chan] = first.astype(LOW)
            second = first * (p[:, n * chan:(n + 1) * chan] * (1.0 - sig))
            plow[flat, (n + 1) * chan:(n + 2) * chan] = second.astype(LOW)
        plow[flat, 4 * chan:] = gate_grad[rng].reshape(-1, chan)
        gu = dot(plow[flat], proj[...], 1, 1)
        nin[0] += eights(gu * hat)
        nin[1] += eights(gu)
        g = g_ref[rng].astype(F32).reshape(-1, chan)
        grad_z = g + norm_back(gu * norms[0:1], hat, inverse)
        out[rng] = grad_z.astype(LOW).reshape(sub, nk, chan)
        return 0

    lax.fori_loop(0, rows // sub, step, 0, unroll=rows // sub)
    wproj[...] += dot(ulow[...], plow[...], 0, 0)


def input_call(z, g, gleft, keep, got, gate_grad, norms, proj, rowm, colm, nblocks, h, parts,
               micros, token):
    tokens = [] if token is None else [token]
    ni, nk, chan = z.shape
    nrow = ni // nblocks
    rows = nrow // 4
    sub = rows // 2
    per = 4 // parts
    flat = pl.BlockSpec((rows, nk, chan), lambda s, r: (s * 4 + h * per + r, 0, 0))
    mask = pl.BlockSpec((1, rows, chan), lambda s, r: (s * 4 + h * per + r, 0, 0))
    rowm = rowm.reshape(-1, rows, chan)
    width = proj.shape[1]
    sums = [sds((chan, width), F32), sds((2, 8, chan), F32)]
    whole = lambda v: pl.BlockSpec(v.shape, lambda s, r: (0,) * len(v.shape))
    return pl.pallas_call(
        lambda *refs: input_kernel(sub, *refs[:10], *refs[10 + len(tokens):]),
        grid=(nblocks, per),
        in_specs=[flat] * 6 + [whole(norms), whole(proj), mask, whole(colm)]
        + [pl.BlockSpec(memory_space=pl.ANY)] * len(tokens),
        out_specs=[pl.BlockSpec((rows, nk, chan), lambda s, r: (s * per + r, 0, 0))]
        + [whole(v) for v in sums],
        out_shape=[sds((ni // parts, nk, chan), LOW)] + sums,
        scratch_shapes=[pltpu.VMEM((rows * nk, chan), LOW), pltpu.VMEM((rows * nk, width), LOW)],
        compiler_params=params(58),
        cost_estimate=cost(micros),
        name="input_grad",
    )(z, g, gleft, keep, got, gate_grad, norms, proj, rowm, colm, *tokens)


def place_call(blocks, b, batches, h, parts, whole=None):
    count, size, nk, chan = blocks.shape

    def kernel(*refs):
        refs[-2][...] = refs[0][...]
        refs[-1][...] = jnp.zeros_like(refs[-1])

    args = [blocks] + ([] if whole is None else [whole])
    return pl.pallas_call(
        kernel,
        grid=(count, 2),
        in_specs=[pl.BlockSpec((1, size // 2, nk, chan), lambda g, r: (g, r, 0, 0))]
        + [pl.BlockSpec(memory_space=pl.ANY)] * (len(args) - 1),
        out_specs=[pl.BlockSpec((1, size // 2, nk, chan),
                                lambda g, r: (b * count + g, h * 2 + r, 0, 0)),
                   pl.BlockSpec((8, 128), lambda g, r: (0, 0))],
        out_shape=[sds((count * batches, size * parts, nk, chan), LOW), sds((8, 128), F32)],
        input_output_aliases={} if whole is None else {1: 0},
        compiler_params=params(58),
        cost_estimate=cost(0.02),
        name="place",
    )(*args)


def shards(rows, cols, pair, cotangent, residue_mask, weights, norm_params, momentum,
           norm_momentum, average, norm_average):
    zeds = rows // 2
    crops, nrow, ncol, chan = pair.shape
    batches = crops // zeds
    length = residue_mask.shape[1]
    ni = zeds * nrow
    row = lax.axis_index("row")
    col = lax.axis_index("col")
    zed, core = row // 2, row % 2
    weight_low = weights.astype(LOW)
    project_low = jnp.concatenate([weight_low[n] for n in range(5)], axis=1)
    mask_float = residue_mask.astype(F32)
    scal = jnp.stack([core]).astype(jnp.int32)
    same_core = [[2 * q + c for q in range(zeds)] for c in range(2)]

    def zswap(blocks):
        return lax.all_to_all(blocks, "row", 0, 0, tiled=True, axis_index_groups=same_core)

    def coreswap(block):
        return lax.ppermute(block, "row", [(r, r ^ 1) for r in range(rows)])

    def after(values, *others):
        return lax.optimization_barrier((values, others))[0]

    def flat(v):
        return v.reshape(ni, ncol, chan)

    def blocked(v):
        return v.reshape(zeds, nrow, ncol, chan)

    def sum_col(term):
        count = term.shape[0] // 2
        mine = lax.dynamic_slice_in_dim(term, core * count, count, 0)
        mine = mine + coreswap(lax.dynamic_slice_in_dim(term, (1 - core) * count, count, 0))
        step = 1
        while step < cols:
            mine = mine + lax.ppermute(mine, "col", [(q, q ^ step) for q in range(cols)])
            step *= 2
        return mine

    def sum_zed(mine, second, third):
        step = 2
        while step < rows:
            if step * 2 >= rows:
                mine = mine + second[:1]
            mine = mine + lax.ppermute(mine, "row", [(r, r ^ step) for r in range(rows)])
            step *= 2
        mine = mine + third[:1]
        got = coreswap(mine)
        return jnp.concatenate([jnp.where(core == 0, mine, got), jnp.where(core == 0, got, mine)])

    masks = []
    for b in range(batches):
        crop_mask = lax.dynamic_index_in_dim(mask_float, b * zeds + zed, 0, keepdims=False)
        by_block = crop_mask.reshape(zeds, 2, nrow)
        rowm = lax.dynamic_index_in_dim(by_block, core, 1, keepdims=False).reshape(-1)
        colm = lax.dynamic_slice_in_dim(crop_mask, col * ncol, ncol, 0)
        masks.append((jnp.broadcast_to(rowm[:, None], (ni, chan)),
                      jnp.broadcast_to(colm[:, None], (ncol, chan))))

    def take(whole, b):
        return whole[b * zeds:(b + 1) * zeds]

    def edges(b):
        left, right = edges_call(pairs[b], norm_params, project_low[:, :4 * chan], *masks[b])
        return left, right, coreswap(right)

    pairs, cots, kept, reduced = [], [], [], []
    last = None
    for b in range(batches):
        block = take(after(pair, block), b) if b else take(pair, b)
        last = zswap(after(block, last) if b else block)
        pairs.append(flat(last))
    sliced = [take(cotangent, b) for b in range(batches)]
    pairs[0] = after(pairs[0], sliced)
    for b in range(batches):
        last = zswap(after(sliced[b], last))
        cots.append(flat(last))
    for b in range(batches):
        if b:
            pairs[b] = after(pairs[b], part)
        left, right, other = edges(b)
        kept.append((left, right, other))
        part = product_call(scal, left, right, other, cols, 33 if b else 3)
        ready = after(part, reduced[b - 1], cots[b - 1]) if b else part
        reduced.append(flat(lax.psum_scatter(ready, "col", scatter_dimension=0, tiled=True)))
    def collect(pieces, whole=None):
        token = None
        for blocks, b, h, share in pieces:
            whole, token = place_call(blocks, b, batches, h, share, whole)
        return whole, token

    gathered, news, gates, sums = [], [], [], []
    for b in range(batches):
        new, gx, gate_grad, wout, nout = middle_call(
            pairs[b], cots[b], reduced[b], norm_params, weight_low[4], weight_low[5])
        last = zswap(after(blocked(new), last))
        news.append((last, b, 0, 1))
        ready = after(gx, (gathered[b - 1], last) if b else reduced[-1])
        gathered.append(lax.all_gather(ready, "col", axis=0))
        gates.append(gate_grad)
        sums.append((wout, nout))
    new_pair, placed = collect(news)
    term, pair_grad, placed_back = 0.0, None, None
    for b in range(batches):
        final = b == batches - 1
        wout, nout = sums[b]
        grad = after(gathered[b], out) if b else gathered[b]
        gleft, keep, send = edge_grad_call(scal, *kept[b], grad, placed if b else None)
        got = coreswap(send)
        if b:
            got = after(got, last)
        share = 2 if final else 1
        backs = []
        for h in range(share):
            out = input_call(pairs[b], cots[b], gleft, keep, got, gates[b], norm_params,
                             project_low, *masks[b], zeds, h, share, 27 if final else 5,
                             placed_back)
            back, wproj, nin = out
            wproj = jnp.transpose(wproj.reshape(chan, 5, chan), (1, 0, 2)).reshape(5 * chan, chan)
            part = [wproj, jnp.zeros_like(wout) if h else wout, jnp.sum(nin, axis=1),
                    jnp.zeros((2, chan), F32) if h else jnp.sum(nout, axis=1)]
            term = term + jnp.concatenate(part, axis=0)
            back = back.reshape(zeds, nrow // share, ncol, chan)
            if final and h == share - 1:
                term = sum_col(term)
                back = after(back, term)
            last = zswap(after(back, last))
            backs.append((last, b, h, share))
        if not final:
            pair_grad, placed_back = collect(backs, pair_grad)
    pair_grad, second = collect(backs[:1], pair_grad)
    pair_grad, third = collect(backs[1:], pair_grad)
    grads = sum_zed(after(term, backs[0][0]), second, third)
    grad_weights = grads[: 6 * chan].reshape(weights.shape)
    grad_norms = grads[6 * chan:]
    rate = 0.1 / (length * math.sqrt(crops))
    new_momentum = MOMENT * momentum + grad_weights
    new_weights = weights - rate * (grad_weights + MOMENT * new_momentum)
    new_average = DECAY * average + (1.0 - DECAY) * new_weights
    new_norm_momentum = MOMENT * norm_momentum + grad_norms
    new_norms = norm_params - rate * (grad_norms + MOMENT * new_norm_momentum)
    new_norm_average = DECAY * norm_average + (1.0 - DECAY) * new_norms
    return (new_pair, pair_grad, new_weights, new_momentum, new_average, new_norms,
            new_norm_momentum, new_norm_average)


def solution(mesh):
    rows, cols = mesh.shape["row"], mesh.shape["col"]
    tiled = P(None, "row", "col", None)

    def body(*args):
        return shards(rows, cols, *args)

    return jax.shard_map(
        body,
        mesh=mesh,
        in_specs=(tiled, tiled) + (P(),) * 7,
        out_specs=(tiled, tiled) + (P(),) * 6,
        check_vma=False,
    )
```

```python
import math

import jax
import jax.numpy as jnp
from jax import lax
from jax.experimental import pallas as pl
from jax.experimental.pallas import tpu as pltpu
from jax.sharding import PartitionSpec as P

EPS = 1e-05
MOMENT = 0.9
DECAY = 0.8
LOW = jnp.bfloat16
F32 = jnp.float32
MIB = 1 << 20
SHARE = 6_000_000_000


def sds(shape, dtype):
    return jax.ShapeDtypeStruct(shape, dtype)


def params(mib):
    return pltpu.CompilerParams(vmem_limit_bytes=mib * MIB)


def cost(micros):
    return pl.CostEstimate(flops=int(micros * SHARE), bytes_accessed=0, transcendentals=0)


def sigmoid(v):
    return 0.5 * jnp.tanh(0.5 * v) + 0.5


def normalize(v):
    center = v - jnp.mean(v, axis=-1, keepdims=True)
    inverse = lax.rsqrt(jnp.mean(center * center, axis=-1, keepdims=True) + EPS)
    return center * inverse, inverse


def norm_back(grad_hat, normed, inverse):
    first = jnp.mean(grad_hat, axis=-1, keepdims=True)
    second = jnp.mean(grad_hat * normed, axis=-1, keepdims=True)
    return inverse * (grad_hat - first - normed * second)


def dot(a, b, ca=1, cb=0):
    return lax.dot_general(a, b, (((ca,), (cb,)), ((), ())), preferred_element_type=F32)


def eights(v):
    return jnp.sum(v.reshape(-1, 8, v.shape[-1]), axis=0)


def to_major(v):
    return jnp.swapaxes(jnp.swapaxes(v, 1, 2), 0, 1)


def to_minor(v):
    return jnp.swapaxes(jnp.swapaxes(v, 0, 1), 1, 2)


def row_mask(rowm, colm, start, count):
    m = rowm[pl.ds(start, count)][:, None, :] * colm[...][None]
    return m.reshape(-1, m.shape[-1])


def pick_rows(nrow):
    return 16 if nrow % 16 == 0 else 8


def whole_spec(array):
    return pl.BlockSpec(array.shape, lambda s: (0,) * len(array.shape))


def edges_kernel(sub, z_ref, norms, proj, rowm, colm, left, right):
    rows, nk, chan = z_ref.shape
    base = pl.program_id(0) * rows

    def step(t, _):
        at = t * sub
        z = z_ref[pl.ds(at, sub)].astype(F32).reshape(-1, chan)
        hat, _ = normalize(z)
        u = (hat * norms[0:1] + norms[1:2]).astype(LOW)
        p = dot(u, proj[...])
        m = row_mask(rowm, colm, base + at, sub)
        lv = sigmoid(p[:, chan:2 * chan]) * p[:, :chan] * m
        rv = sigmoid(p[:, 3 * chan:]) * p[:, 2 * chan:3 * chan] * m
        left[pl.ds(at, sub)] = lv.astype(LOW).reshape(sub, nk, chan)
        right[pl.ds(at, sub)] = rv.astype(LOW).reshape(sub, nk, chan)
        return 0

    lax.fori_loop(0, rows // sub, step, 0, unroll=rows // sub)


def edges_call(z, norms, proj, rowm, colm):
    ni, nk, chan = z.shape
    rows = 32
    flat = pl.BlockSpec((rows, nk, chan), lambda s: (s, 0, 0))
    return pl.pallas_call(
        lambda *refs: edges_kernel(8, *refs),
        grid=(ni // rows,),
        in_specs=[flat] + [whole_spec(v) for v in (norms, proj, rowm, colm)],
        out_specs=[flat, flat],
        out_shape=[sds(z.shape, LOW)] * 2,
        compiler_params=params(58),
        cost_estimate=cost(27),
        name="edges",
    )(z, norms, proj, rowm, colm)


def product_kernel(nparts, unroll, sc, left, own, other, out, lt, rt, xt):
    s = pl.program_id(0)
    steps = pl.num_programs(0) // 2
    rows, nk, chan = left.shape
    nrow = out.shape[2] // 2
    half = nparts * nrow
    core = sc[0]

    @pl.when(s < steps)
    def _():
        at = pl.multiple_of(s * rows, rows)
        lt[:, pl.ds(at, rows), :] = to_major(left[...])
        rt[:, pl.ds(pl.multiple_of(core * half + at, rows), rows), :] = to_major(own[...])
        rt[:, pl.ds(pl.multiple_of((1 - core) * half + at, rows), rows), :] = to_major(other[...])

    @pl.when(s == steps)
    def _():
        def multiply(c, _):
            xt[c] = dot(lt[c], rt[c], 1, 1).astype(LOW)
            return 0
        lax.fori_loop(0, chan, multiply, 0, unroll=unroll)

    @pl.when(s >= steps)
    def _():
        x = to_minor(xt[:, pl.ds(pl.multiple_of((s - steps) * rows, rows), rows), :])
        for q in range(nparts):
            for c in range(2):
                start = c * half + q * nrow
                out[q, :, c * nrow:(c + 1) * nrow] = x[:, start:start + nrow]


def phases(ni, rows):
    steps = ni // rows
    inward = lambda s: jnp.minimum(s, steps - 1)
    outward = lambda s: jnp.maximum(s - steps, 0)
    return steps, inward, outward


def product_call(scal, left, own, other, nparts, micros):
    ni, nk, chan = left.shape
    nrow = ni // nparts
    nj = 2 * ni
    rows = pick_rows(nrow)
    steps, inward, outward = phases(ni, rows)
    edge = pl.BlockSpec((rows, nk, chan), lambda s, sc: (inward(s), 0, 0))
    return pl.pallas_call(
        lambda *refs: product_kernel(nparts, 16, *refs),
        grid_spec=pltpu.PrefetchScalarGridSpec(
            num_scalar_prefetch=1,
            grid=(2 * steps,),
            in_specs=[edge] * 3,
            out_specs=pl.BlockSpec((nparts, rows, 2 * nrow, chan),
                                   lambda s, sc: (0, outward(s), 0, 0)),
            scratch_shapes=[pltpu.VMEM((chan, ni, nk), LOW), pltpu.VMEM((chan, nj, nk), LOW),
                            pltpu.VMEM((chan, ni, nj), LOW)],
        ),
        out_shape=sds((nparts, ni, 2 * nrow, chan), LOW),
        compiler_params=params(58),
        cost_estimate=cost(micros),
        name="product",
    )(scal, left, own, other)


def middle_kernel(sub, z_ref, g_ref, x_ref, norms, gate_w, out_w, new, gx, gate_grad, wout, nout,
                  ylow, glow):
    rows, nk, chan = z_ref.shape

    @pl.when(pl.program_id(0) == 0)
    def _():
        wout[...] = jnp.zeros_like(wout)
        nout[...] = jnp.zeros_like(nout)

    def step(t, _):
        rng = pl.ds(t * sub, sub)
        flat = pl.ds(pl.multiple_of(t * sub * nk, sub * nk), sub * nk)
        z = z_ref[rng].astype(F32).reshape(-1, chan)
        zhat, _ = normalize(z)
        u = (zhat * norms[0:1] + norms[1:2]).astype(LOW)
        gate = sigmoid(dot(u, gate_w[...]))
        hat, inverse = normalize(x_ref[rng].astype(F32).reshape(-1, chan))
        y = (hat * norms[2:3] + norms[3:4]).astype(LOW)
        out = dot(y, out_w[...])
        so = gate * out
        new[rng] = (z + so).astype(LOW).reshape(sub, nk, chan)
        g = g_ref[rng].astype(F32).reshape(-1, chan)
        go = (g * gate).astype(LOW)
        gate_grad[rng] = (g * so * (1.0 - gate)).astype(LOW).reshape(sub, nk, chan)
        ylow[flat] = y
        glow[flat] = go
        gy = dot(go, out_w[...], 1, 1)
        nout[0] += eights(gy * hat)
        nout[1] += eights(gy)
        gx[rng] = norm_back(gy * norms[2:3], hat, inverse).astype(LOW).reshape(sub, nk, chan)
        return 0

    lax.fori_loop(0, rows // sub, step, 0, unroll=rows // sub)
    wout[...] += dot(ylow[...], glow[...], 0, 0)


def middle_call(z, g, x, norms, gate_w, out_w):
    ni, nk, chan = z.shape
    rows = 16
    flat = pl.BlockSpec((rows, nk, chan), lambda s: (s, 0, 0))
    low = pltpu.VMEM((rows * nk, chan), LOW)
    sums = [sds((chan, chan), F32), sds((2, 8, chan), F32)]
    return pl.pallas_call(
        lambda *refs: middle_kernel(8, *refs),
        grid=(ni // rows,),
        in_specs=[flat] * 3 + [whole_spec(v) for v in (norms, gate_w, out_w)],
        out_specs=[flat] * 3 + [whole_spec(v) for v in sums],
        out_shape=[sds(z.shape, LOW)] * 3 + sums,
        scratch_shapes=[low, low],
        compiler_params=params(58),
        cost_estimate=cost(40),
        name="middle",
    )(z, g, x, norms, gate_w, out_w)


def edge_grad_kernel(nparts, unroll, sc, left, own, other, gxs, gleft, keep, send, lt, rt, gt,
                     gtile):
    s = pl.program_id(0)
    steps = pl.num_programs(0) // 2
    rows, nk, chan = left.shape
    nrow = gtile.shape[1] // 2
    gxs = [v.at[0] for v in gxs]
    half = nparts * nrow
    core = sc[0]

    @pl.when(s < steps)
    def _():
        at = pl.multiple_of(s * rows, rows)
        lt[:, pl.ds(at, rows), :] = to_major(left[...])
        rt[:, pl.ds(pl.multiple_of(core * half + at, rows), rows), :] = to_major(own[...])
        rt[:, pl.ds(pl.multiple_of((1 - core) * half + at, rows), rows), :] = to_major(other[...])
        tiles = gxs
        if len(gxs) > nparts:
            for h in range(2):
                @pl.when((s >= steps // 2) if h else (s < steps // 2))
                def _(h=h):
                    gtile[...] = gxs[nparts - 1 + h][...]
            tiles = gxs[:nparts - 1] + [gtile]
        g = jnp.concatenate([
            tiles[q][:, c * nrow:(c + 1) * nrow] for c in range(2) for q in range(nparts)
        ], axis=1)
        gt[:, pl.ds(at, rows), :] = to_major(g)

    @pl.when(s == steps)
    def _():
        def multiply(c, _):
            lc, rc, gc = lt[c], rt[c], gt[c]
            lt[c] = dot(gc, rc, 1, 0).astype(LOW)
            rt[c] = dot(gc, lc, 0, 0).astype(LOW)
            return 0
        lax.fori_loop(0, chan, multiply, 0, unroll=unroll)

    @pl.when(s >= steps)
    def _():
        at = pl.multiple_of((s - steps) * rows, rows)
        gleft[...] = to_minor(lt[:, pl.ds(at, rows), :])
        keep[...] = to_minor(rt[:, pl.ds(pl.multiple_of(core * half + at, rows), rows), :])
        send[...] = to_minor(rt[:, pl.ds(pl.multiple_of((1 - core) * half + at, rows), rows), :])


def edge_grad_call(scal, left, own, other, gxs, token):
    tokens = [] if token is None else [token]
    ni, nk, chan = left.shape
    nj = 2 * ni
    nparts = nj // gxs[0].shape[-2]
    nrow = ni // nparts
    rows = pick_rows(nrow)
    per = nrow // rows
    steps, inward, outward = phases(ni, rows)
    edge = pl.BlockSpec((rows, nk, chan), lambda s, sc: (inward(s), 0, 0))
    part = lambda way: pl.BlockSpec(
        (rows, nk, chan), lambda s, sc: (sc[1 + way(s) // per] * per + way(s) % per, 0, 0))
    back = pl.BlockSpec((rows, nk, chan), lambda s, sc: (outward(s), 0, 0))
    block = (1, rows, 2 * nrow, chan)
    if len(gxs) == 1:
        specs = [pl.BlockSpec(block, lambda s, sc, q=q: (q, inward(s), 0, 0))
                 for q in range(nparts)]
        gxs = gxs * nparts
    else:
        gxs = [v[None] for v in gxs]
        specs = [pl.BlockSpec(block, lambda s, sc: (0, inward(s), 0, 0))] * (nparts - 1)
        specs += [pl.BlockSpec(block, lambda s, sc, h=h: (
            0, jnp.clip(s - h * (steps // 2), 0, steps // 2 - 1), 0, 0)) for h in range(2)]
    count = len(gxs)
    return pl.pallas_call(
        lambda *refs: edge_grad_kernel(nparts, 16, *refs[:4], refs[4:4 + count],
                                       *refs[4 + count + len(tokens):]),
        grid_spec=pltpu.PrefetchScalarGridSpec(
            num_scalar_prefetch=1,
            grid=(2 * steps,),
            in_specs=[edge, part(inward), part(inward)] + specs
            + [pl.BlockSpec(memory_space=pl.ANY)] * len(tokens),
            out_specs=[back, part(outward), part(outward)],
            scratch_shapes=[pltpu.VMEM((chan, ni, nk), LOW), pltpu.VMEM((chan, nj, nk), LOW),
                            pltpu.VMEM((chan, ni, nj), LOW),
                            pltpu.VMEM((rows, 2 * nrow, chan), LOW)],
        ),
        out_shape=[sds(left.shape, LOW)] * 3,
        compiler_params=params(58),
        cost_estimate=cost(5),
        name="edge_grad",
    )(scal, left, own, other, *gxs, *tokens)


def input_kernel(sub, z_ref, g_ref, gleft, keep, got, gate_grad, norms, proj, rowm, colm,
                 out, wproj, nin, ulow, plow):
    rows, nk, chan = z_ref.shape

    @pl.when((pl.program_id(0) == 0) & (pl.program_id(1) == 0))
    def _():
        wproj[...] = jnp.zeros_like(wproj)
        nin[...] = jnp.zeros_like(nin)

    def step(t, _):
        at = t * sub
        rng = pl.ds(at, sub)
        flat = pl.ds(pl.multiple_of(at * nk, sub * nk), sub * nk)
        z = z_ref[rng].astype(F32).reshape(-1, chan)
        hat, inverse = normalize(z)
        u = (hat * norms[0:1] + norms[1:2]).astype(LOW)
        ulow[flat] = u
        p = dot(u, proj[:, :4 * chan])
        m = row_mask(rowm.at[0], colm, at, sub)
        gl = gleft[rng].astype(F32).reshape(-1, chan) * m
        gr = (keep[rng].astype(F32) + got[rng].astype(F32)).reshape(-1, chan) * m
        for n, grad in ((0, gl), (2, gr)):
            sig = sigmoid(p[:, (n + 1) * chan:(n + 2) * chan])
            first = grad * sig
            plow[flat, n * chan:(n + 1) * chan] = first.astype(LOW)
            second = first * (p[:, n * chan:(n + 1) * chan] * (1.0 - sig))
            plow[flat, (n + 1) * chan:(n + 2) * chan] = second.astype(LOW)
        plow[flat, 4 * chan:] = gate_grad[rng].reshape(-1, chan)
        gu = dot(plow[flat], proj[...], 1, 1)
        nin[0] += eights(gu * hat)
        nin[1] += eights(gu)
        g = g_ref[rng].astype(F32).reshape(-1, chan)
        grad_z = g + norm_back(gu * norms[0:1], hat, inverse)
        out[rng] = grad_z.astype(LOW).reshape(sub, nk, chan)
        return 0

    lax.fori_loop(0, rows // sub, step, 0, unroll=rows // sub)
    wproj[...] += dot(ulow[...], plow[...], 0, 0)


def input_call(z, g, gleft, keep, got, gate_grad, norms, proj, rowm, colm, nblocks, h, parts,
               micros, token):
    tokens = [] if token is None else [token]
    ni, nk, chan = z.shape
    nrow = ni // nblocks
    rows = nrow // 4
    sub = rows // 2
    per = 4 // parts
    flat = pl.BlockSpec((rows, nk, chan), lambda s, r: (s * 4 + h * per + r, 0, 0))
    mask = pl.BlockSpec((1, rows, chan), lambda s, r: (s * 4 + h * per + r, 0, 0))
    rowm = rowm.reshape(-1, rows, chan)
    width = proj.shape[1]
    sums = [sds((chan, width), F32), sds((2, 8, chan), F32)]
    whole = lambda v: pl.BlockSpec(v.shape, lambda s, r: (0,) * len(v.shape))
    return pl.pallas_call(
        lambda *refs: input_kernel(sub, *refs[:10], *refs[10 + len(tokens):]),
        grid=(nblocks, per),
        in_specs=[flat] * 6 + [whole(norms), whole(proj), mask, whole(colm)]
        + [pl.BlockSpec(memory_space=pl.ANY)] * len(tokens),
        out_specs=[pl.BlockSpec((rows, nk, chan), lambda s, r: (s * per + r, 0, 0))]
        + [whole(v) for v in sums],
        out_shape=[sds((ni // parts, nk, chan), LOW)] + sums,
        scratch_shapes=[pltpu.VMEM((rows * nk, chan), LOW), pltpu.VMEM((rows * nk, width), LOW)],
        compiler_params=params(58),
        cost_estimate=cost(micros),
        name="input_grad",
    )(z, g, gleft, keep, got, gate_grad, norms, proj, rowm, colm, *tokens)


def place_call(blocks, b, batches, h, parts, whole=None):
    count, size, nk, chan = blocks.shape

    def kernel(*refs):
        refs[-2][...] = refs[0][...]
        refs[-1][...] = jnp.zeros_like(refs[-1])

    args = [blocks] + ([] if whole is None else [whole])
    return pl.pallas_call(
        kernel,
        grid=(count, 2),
        in_specs=[pl.BlockSpec((1, size // 2, nk, chan), lambda g, r: (g, r, 0, 0))]
        + [pl.BlockSpec(memory_space=pl.ANY)] * (len(args) - 1),
        out_specs=[pl.BlockSpec((1, size // 2, nk, chan),
                                lambda g, r: (b * count + g, h * 2 + r, 0, 0)),
                   pl.BlockSpec((8, 128), lambda g, r: (0, 0))],
        out_shape=[sds((count * batches, size * parts, nk, chan), LOW), sds((8, 128), F32)],
        input_output_aliases={} if whole is None else {1: 0},
        compiler_params=params(58),
        cost_estimate=cost(0.02),
        name="place",
    )(*args)


def shards(rows, cols, pair, cotangent, residue_mask, weights, norm_params, momentum,
           norm_momentum, average, norm_average):
    zeds = rows // 2
    crops, nrow, ncol, chan = pair.shape
    batches = crops // zeds
    length = residue_mask.shape[1]
    ni = zeds * nrow
    row = lax.axis_index("row")
    col = lax.axis_index("col")
    zed, core = row // 2, row % 2
    weight_low = weights.astype(LOW)
    project_low = jnp.concatenate([weight_low[n] for n in range(5)], axis=1)
    mask_float = residue_mask.astype(F32)
    by_column = jnp.stack([core] + list(range(cols))).astype(jnp.int32)
    by_distance = jnp.stack([core] + [col ^ e for e in range(cols)]).astype(jnp.int32)
    near = [b for b in range(batches - 1) if cols == 4]
    same_core = [[2 * q + c for q in range(zeds)] for c in range(2)]

    def zswap(blocks):
        return lax.all_to_all(blocks, "row", 0, 0, tiled=True, axis_index_groups=same_core)

    def coreswap(block):
        return lax.ppermute(block, "row", [(r, r ^ 1) for r in range(rows)])

    def after(values, *others):
        return lax.optimization_barrier((values, others))[0]

    def flat(v):
        return v.reshape(ni, ncol, chan)

    def blocked(v):
        return v.reshape(zeds, nrow, ncol, chan)

    def col_move(v, e):
        return lax.ppermute(v, "col", [(q, q ^ e) for q in range(cols)])

    def gather_near(own):
        return [own, col_move(own, 1), col_move(own, 2)]

    def gather_far(near):
        own, from_x, from_y = near
        half = own.shape[0] // 2
        return near + [col_move(from_y[:half], 1), col_move(from_x[half:], 2)]

    def sum_col(term):
        count = term.shape[0] // 2
        mine = lax.dynamic_slice_in_dim(term, core * count, count, 0)
        mine = mine + coreswap(lax.dynamic_slice_in_dim(term, (1 - core) * count, count, 0))
        step = 1
        while step < cols:
            mine = mine + lax.ppermute(mine, "col", [(q, q ^ step) for q in range(cols)])
            step *= 2
        return mine

    def sum_zed(mine, second, third):
        step = 2
        while step < rows:
            if step * 2 >= rows:
                mine = mine + second[:1]
            mine = mine + lax.ppermute(mine, "row", [(r, r ^ step) for r in range(rows)])
            step *= 2
        mine = mine + third[:1]
        got = coreswap(mine)
        return jnp.concatenate([jnp.where(core == 0, mine, got), jnp.where(core == 0, got, mine)])

    masks = []
    for b in range(batches):
        crop_mask = lax.dynamic_index_in_dim(mask_float, b * zeds + zed, 0, keepdims=False)
        by_block = crop_mask.reshape(zeds, 2, nrow)
        rowm = lax.dynamic_index_in_dim(by_block, core, 1, keepdims=False).reshape(-1)
        colm = lax.dynamic_slice_in_dim(crop_mask, col * ncol, ncol, 0)
        masks.append((jnp.broadcast_to(rowm[:, None], (ni, chan)),
                      jnp.broadcast_to(colm[:, None], (ncol, chan))))

    def take(whole, b):
        return whole[b * zeds:(b + 1) * zeds]

    def edges(b):
        left, right = edges_call(pairs[b], norm_params, project_low[:, :4 * chan], *masks[b])
        return left, right, coreswap(right)

    pairs, cots, kept, reduced = [], [], [], []
    last = None
    for b in range(batches):
        block = take(after(pair, block), b) if b else take(pair, b)
        last = zswap(after(block, last) if b else block)
        pairs.append(flat(last))
    sliced = [take(cotangent, b) for b in range(batches)]
    pairs[0] = after(pairs[0], sliced)
    for b in range(batches):
        last = zswap(after(sliced[b], last))
        cots.append(flat(last))
    for b in range(batches):
        if b:
            pairs[b] = after(pairs[b], part)
        left, right, other = edges(b)
        kept.append((left, right, other))
        part = product_call(by_column, left, right, other, cols, 33 if b else 3)
        ready = after(part, reduced[b - 1], cots[b - 1]) if b else part
        reduced.append(flat(lax.psum_scatter(ready, "col", scatter_dimension=0, tiled=True)))
    def collect(pieces, whole=None):
        token = None
        for blocks, b, h, share in pieces:
            whole, token = place_call(blocks, b, batches, h, share, whole)
        return whole, token

    gathered, news, gates, sums = [], [], [], []
    for b in range(batches):
        new, gx, gate_grad, wout, nout = middle_call(
            pairs[b], cots[b], reduced[b], norm_params, weight_low[4], weight_low[5])
        last = zswap(after(blocked(new), last))
        news.append((last, b, 0, 1))
        ready = after(gx, (gathered[b - 1], last) if b else reduced[-1])
        if b - 1 in near:
            gathered[b - 1] = gather_far(after(gathered[b - 1], gx, news[b - 1][0]))
            ready = after(gx, gathered[b - 1], last)
        if b in near:
            gathered.append(gather_near(ready))
        else:
            gathered.append([lax.all_gather(ready, "col", axis=0)])
        gates.append(gate_grad)
        sums.append((wout, nout))
    new_pair, placed = collect(news)
    term, pair_grad, placed_back = 0.0, None, None
    for b in range(batches):
        final = b == batches - 1
        wout, nout = sums[b]
        grad = after(gathered[b], out) if b else gathered[b]
        if b in near and final:
            grad = gather_far(grad)
        gleft, keep, send = edge_grad_call(by_distance if b in near else by_column, *kept[b], grad, placed if b else None)
        got = coreswap(send)
        if b:
            got = after(got, last)
        share = 2 if final else 1
        backs = []
        for h in range(share):
            out = input_call(pairs[b], cots[b], gleft, keep, got, gates[b], norm_params,
                             project_low, *masks[b], zeds, h, share, 27 if final else 5,
                             placed_back)
            back, wproj, nin = out
            wproj = jnp.transpose(wproj.reshape(chan, 5, chan), (1, 0, 2)).reshape(5 * chan, chan)
            part = [wproj, jnp.zeros_like(wout) if h else wout, jnp.sum(nin, axis=1),
                    jnp.zeros((2, chan), F32) if h else jnp.sum(nout, axis=1)]
            term = term + jnp.concatenate(part, axis=0)
            back = back.reshape(zeds, nrow // share, ncol, chan)
            if final and h == share - 1:
                term = sum_col(term)
                back = after(back, term)
            last = zswap(after(back, last))
            backs.append((last, b, h, share))
        if not final:
            pair_grad, placed_back = collect(backs, pair_grad)
    pair_grad, second = collect(backs[:1], pair_grad)
    pair_grad, third = collect(backs[1:], pair_grad)
    grads = sum_zed(after(term, backs[0][0]), second, third)
    grad_weights = grads[: 6 * chan].reshape(weights.shape)
    grad_norms = grads[6 * chan:]
    rate = 0.1 / (length * math.sqrt(crops))
    new_momentum = MOMENT * momentum + grad_weights
    new_weights = weights - rate * (grad_weights + MOMENT * new_momentum)
    new_average = DECAY * average + (1.0 - DECAY) * new_weights
    new_norm_momentum = MOMENT * norm_momentum + grad_norms
    new_norms = norm_params - rate * (grad_norms + MOMENT * new_norm_momentum)
    new_norm_average = DECAY * norm_average + (1.0 - DECAY) * new_norms
    return (new_pair, pair_grad, new_weights, new_momentum, new_average, new_norms,
            new_norm_momentum, new_norm_average)


def solution(mesh):
    rows, cols = mesh.shape["row"], mesh.shape["col"]
    tiled = P(None, "row", "col", None)

    def body(*args):
        return shards(rows, cols, *args)

    return jax.shard_map(
        body,
        mesh=mesh,
        in_specs=(tiled, tiled) + (P(),) * 7,
        out_specs=(tiled, tiled) + (P(),) * 6,
        check_vma=False,
    )
```

```python
import math

import jax
import jax.numpy as jnp
from jax import lax
from jax.experimental import pallas as pl
from jax.experimental.pallas import tpu as pltpu
from jax.sharding import PartitionSpec as P

EPS = 1e-05
MOMENT = 0.9
DECAY = 0.8
LOW = jnp.bfloat16
F32 = jnp.float32
MIB = 1 << 20
SHARE = 6_000_000_000


def sds(shape, dtype):
    return jax.ShapeDtypeStruct(shape, dtype)


def params(mib):
    return pltpu.CompilerParams(vmem_limit_bytes=mib * MIB)


def cost(micros):
    return pl.CostEstimate(flops=int(micros * SHARE), bytes_accessed=0, transcendentals=0)


def sigmoid(v):
    return 0.5 * jnp.tanh(0.5 * v) + 0.5


def normalize(v):
    center = v - jnp.mean(v, axis=-1, keepdims=True)
    inverse = lax.rsqrt(jnp.mean(center * center, axis=-1, keepdims=True) + EPS)
    return center * inverse, inverse


def norm_back(grad_hat, normed, inverse):
    first = jnp.mean(grad_hat, axis=-1, keepdims=True)
    second = jnp.mean(grad_hat * normed, axis=-1, keepdims=True)
    return inverse * (grad_hat - first - normed * second)


def dot(a, b, ca=1, cb=0):
    return lax.dot_general(a, b, (((ca,), (cb,)), ((), ())), preferred_element_type=F32)


def eights(v):
    return jnp.sum(v.reshape(-1, 8, v.shape[-1]), axis=0)


def to_major(v):
    return jnp.swapaxes(jnp.swapaxes(v, 1, 2), 0, 1)


def to_minor(v):
    return jnp.swapaxes(jnp.swapaxes(v, 0, 1), 1, 2)


def row_mask(rowm, colm, start, count):
    m = rowm[pl.ds(start, count)][:, None, :] * colm[...][None]
    return m.reshape(-1, m.shape[-1])


def pick_rows(nrow):
    return 16 if nrow % 16 == 0 else 8


def whole_spec(array):
    return pl.BlockSpec(array.shape, lambda s: (0,) * len(array.shape))


def edges_kernel(sub, z_ref, norms, proj, rowm, colm, left, right):
    rows, nk, chan = z_ref.shape
    base = pl.program_id(0) * rows

    def step(t, _):
        at = t * sub
        z = z_ref[pl.ds(at, sub)].astype(F32).reshape(-1, chan)
        hat, _ = normalize(z)
        u = (hat * norms[0:1] + norms[1:2]).astype(LOW)
        p = dot(u, proj[...])
        m = row_mask(rowm, colm, base + at, sub)
        lv = sigmoid(p[:, chan:2 * chan]) * p[:, :chan] * m
        rv = sigmoid(p[:, 3 * chan:]) * p[:, 2 * chan:3 * chan] * m
        left[pl.ds(at, sub)] = lv.astype(LOW).reshape(sub, nk, chan)
        right[pl.ds(at, sub)] = rv.astype(LOW).reshape(sub, nk, chan)
        return 0

    lax.fori_loop(0, rows // sub, step, 0, unroll=rows // sub)


def edges_call(z, norms, proj, rowm, colm):
    ni, nk, chan = z.shape
    rows = 32
    flat = pl.BlockSpec((rows, nk, chan), lambda s: (s, 0, 0))
    return pl.pallas_call(
        lambda *refs: edges_kernel(8, *refs),
        grid=(ni // rows,),
        in_specs=[flat] + [whole_spec(v) for v in (norms, proj, rowm, colm)],
        out_specs=[flat, flat],
        out_shape=[sds(z.shape, LOW)] * 2,
        compiler_params=params(58),
        cost_estimate=cost(27),
        name="edges",
    )(z, norms, proj, rowm, colm)


def product_kernel(nparts, unroll, sc, left, own, other, out, lt, rt, xt):
    s = pl.program_id(0)
    steps = pl.num_programs(0) // 2
    rows, nk, chan = left.shape
    nrow = out.shape[2] // 2
    half = nparts * nrow
    core = sc[0]

    @pl.when(s < steps)
    def _():
        at = pl.multiple_of(s * rows, rows)
        lt[:, pl.ds(at, rows), :] = to_major(left[...])
        rt[:, pl.ds(pl.multiple_of(core * half + at, rows), rows), :] = to_major(own[...])
        rt[:, pl.ds(pl.multiple_of((1 - core) * half + at, rows), rows), :] = to_major(other[...])

    @pl.when(s == steps)
    def _():
        def multiply(c, _):
            xt[c] = dot(lt[c], rt[c], 1, 1).astype(LOW)
            return 0
        lax.fori_loop(0, chan, multiply, 0, unroll=unroll)

    @pl.when(s >= steps)
    def _():
        x = to_minor(xt[:, pl.ds(pl.multiple_of((s - steps) * rows, rows), rows), :])
        for q in range(nparts):
            for c in range(2):
                start = c * half + q * nrow
                out[q, :, c * nrow:(c + 1) * nrow] = x[:, start:start + nrow]


def phases(ni, rows):
    steps = ni // rows
    inward = lambda s: jnp.minimum(s, steps - 1)
    outward = lambda s: jnp.maximum(s - steps, 0)
    return steps, inward, outward


def product_call(scal, left, own, other, nparts, micros):
    ni, nk, chan = left.shape
    nrow = ni // nparts
    nj = 2 * ni
    rows = pick_rows(nrow)
    steps, inward, outward = phases(ni, rows)
    edge = pl.BlockSpec((rows, nk, chan), lambda s, sc: (inward(s), 0, 0))
    return pl.pallas_call(
        lambda *refs: product_kernel(nparts, 16, *refs),
        grid_spec=pltpu.PrefetchScalarGridSpec(
            num_scalar_prefetch=1,
            grid=(2 * steps,),
            in_specs=[edge] * 3,
            out_specs=pl.BlockSpec((nparts, rows, 2 * nrow, chan),
                                   lambda s, sc: (0, outward(s), 0, 0)),
            scratch_shapes=[pltpu.VMEM((chan, ni, nk), LOW), pltpu.VMEM((chan, nj, nk), LOW),
                            pltpu.VMEM((chan, ni, nj), LOW)],
        ),
        out_shape=sds((nparts, ni, 2 * nrow, chan), LOW),
        compiler_params=params(58),
        cost_estimate=cost(micros),
        name="product",
    )(scal, left, own, other)


def middle_kernel(sub, z_ref, g_ref, x_ref, norms, gate_w, out_w, new, gx, gate_grad, wout, nout,
                  ylow, glow):
    rows, nk, chan = z_ref.shape

    @pl.when(pl.program_id(0) == 0)
    def _():
        wout[...] = jnp.zeros_like(wout)
        nout[...] = jnp.zeros_like(nout)

    def step(t, _):
        rng = pl.ds(t * sub, sub)
        flat = pl.ds(pl.multiple_of(t * sub * nk, sub * nk), sub * nk)
        z = z_ref[rng].astype(F32).reshape(-1, chan)
        zhat, _ = normalize(z)
        u = (zhat * norms[0:1] + norms[1:2]).astype(LOW)
        gate = sigmoid(dot(u, gate_w[...]))
        hat, inverse = normalize(x_ref[rng].astype(F32).reshape(-1, chan))
        y = (hat * norms[2:3] + norms[3:4]).astype(LOW)
        out = dot(y, out_w[...])
        so = gate * out
        new[rng] = (z + so).astype(LOW).reshape(sub, nk, chan)
        g = g_ref[rng].astype(F32).reshape(-1, chan)
        go = (g * gate).astype(LOW)
        gate_grad[rng] = (g * so * (1.0 - gate)).astype(LOW).reshape(sub, nk, chan)
        ylow[flat] = y
        glow[flat] = go
        gy = dot(go, out_w[...], 1, 1)
        nout[0] += eights(gy * hat)
        nout[1] += eights(gy)
        gx[rng] = norm_back(gy * norms[2:3], hat, inverse).astype(LOW).reshape(sub, nk, chan)
        return 0

    lax.fori_loop(0, rows // sub, step, 0, unroll=rows // sub)
    wout[...] += dot(ylow[...], glow[...], 0, 0)


def middle_call(z, g, x, norms, gate_w, out_w):
    ni, nk, chan = z.shape
    rows = 16
    flat = pl.BlockSpec((rows, nk, chan), lambda s: (s, 0, 0))
    low = pltpu.VMEM((rows * nk, chan), LOW)
    sums = [sds((chan, chan), F32), sds((2, 8, chan), F32)]
    return pl.pallas_call(
        lambda *refs: middle_kernel(8, *refs),
        grid=(ni // rows,),
        in_specs=[flat] * 3 + [whole_spec(v) for v in (norms, gate_w, out_w)],
        out_specs=[flat] * 3 + [whole_spec(v) for v in sums],
        out_shape=[sds(z.shape, LOW)] * 3 + sums,
        scratch_shapes=[low, low],
        compiler_params=params(58),
        cost_estimate=cost(40),
        name="middle",
    )(z, g, x, norms, gate_w, out_w)


def edge_grad_kernel(nparts, unroll, sc, left, own, other, gxs, gleft, keep, send, lt, rt, gt,
                     gtile):
    s = pl.program_id(0)
    steps = pl.num_programs(0) // 2
    rows, nk, chan = left.shape
    nrow = gtile.shape[1] // 2
    gxs = [v.at[0] for v in gxs]
    half = nparts * nrow
    core = sc[0]

    @pl.when(s < steps)
    def _():
        at = pl.multiple_of(s * rows, rows)
        lt[:, pl.ds(at, rows), :] = to_major(left[...])
        rt[:, pl.ds(pl.multiple_of(core * half + at, rows), rows), :] = to_major(own[...])
        rt[:, pl.ds(pl.multiple_of((1 - core) * half + at, rows), rows), :] = to_major(other[...])
        tiles = gxs
        if len(gxs) > nparts:
            for h in range(2):
                @pl.when((s >= steps // 2) if h else (s < steps // 2))
                def _(h=h):
                    gtile[...] = gxs[nparts - 1 + h][...]
            tiles = gxs[:nparts - 1] + [gtile]
        g = jnp.concatenate([
            tiles[q][:, c * nrow:(c + 1) * nrow] for c in range(2) for q in range(nparts)
        ], axis=1)
        gt[:, pl.ds(at, rows), :] = to_major(g)

    @pl.when(s == steps)
    def _():
        def multiply(c, _):
            lc, rc, gc = lt[c], rt[c], gt[c]
            lt[c] = dot(gc, rc, 1, 0).astype(LOW)
            rt[c] = dot(gc, lc, 0, 0).astype(LOW)
            return 0
        lax.fori_loop(0, chan, multiply, 0, unroll=unroll)

    @pl.when(s >= steps)
    def _():
        at = pl.multiple_of((s - steps) * rows, rows)
        gleft[...] = to_minor(lt[:, pl.ds(at, rows), :])
        keep[...] = to_minor(rt[:, pl.ds(pl.multiple_of(core * half + at, rows), rows), :])
        send[...] = to_minor(rt[:, pl.ds(pl.multiple_of((1 - core) * half + at, rows), rows), :])


def edge_grad_call(scal, left, own, other, gxs, token):
    tokens = [] if token is None else [token]
    ni, nk, chan = left.shape
    nj = 2 * ni
    nparts = nj // gxs[0].shape[-2]
    nrow = ni // nparts
    rows = pick_rows(nrow)
    per = nrow // rows
    steps, inward, outward = phases(ni, rows)
    edge = pl.BlockSpec((rows, nk, chan), lambda s, sc: (inward(s), 0, 0))
    part = lambda way: pl.BlockSpec(
        (rows, nk, chan), lambda s, sc: (sc[1 + way(s) // per] * per + way(s) % per, 0, 0))
    back = pl.BlockSpec((rows, nk, chan), lambda s, sc: (outward(s), 0, 0))
    block = (1, rows, 2 * nrow, chan)
    if len(gxs) == 1:
        specs = [pl.BlockSpec(block, lambda s, sc, q=q: (q, inward(s), 0, 0))
                 for q in range(nparts)]
        gxs = gxs * nparts
    else:
        gxs = [v[None] for v in gxs]
        specs = [pl.BlockSpec(block, lambda s, sc: (0, inward(s), 0, 0))] * (nparts - 1)
        specs += [pl.BlockSpec(block, lambda s, sc, h=h: (
            0, jnp.clip(s - h * (steps // 2), 0, steps // 2 - 1), 0, 0)) for h in range(2)]
    count = len(gxs)
    return pl.pallas_call(
        lambda *refs: edge_grad_kernel(nparts, 16, *refs[:4], refs[4:4 + count],
                                       *refs[4 + count + len(tokens):]),
        grid_spec=pltpu.PrefetchScalarGridSpec(
            num_scalar_prefetch=1,
            grid=(2 * steps,),
            in_specs=[edge, part(inward), part(inward)] + specs
            + [pl.BlockSpec(memory_space=pl.ANY)] * len(tokens),
            out_specs=[back, part(outward), part(outward)],
            scratch_shapes=[pltpu.VMEM((chan, ni, nk), LOW), pltpu.VMEM((chan, nj, nk), LOW),
                            pltpu.VMEM((chan, ni, nj), LOW),
                            pltpu.VMEM((rows, 2 * nrow, chan), LOW)],
        ),
        out_shape=[sds(left.shape, LOW)] * 3,
        compiler_params=params(58),
        cost_estimate=cost(5),
        name="edge_grad",
    )(scal, left, own, other, *gxs, *tokens)


def input_kernel(sub, z_ref, g_ref, gleft, keep, got, gate_grad, norms, proj, rowm, colm,
                 out, wproj, nin, ulow, plow):
    rows, nk, chan = z_ref.shape

    @pl.when((pl.program_id(0) == 0) & (pl.program_id(1) == 0))
    def _():
        wproj[...] = jnp.zeros_like(wproj)
        nin[...] = jnp.zeros_like(nin)

    def step(t, _):
        at = t * sub
        rng = pl.ds(at, sub)
        flat = pl.ds(pl.multiple_of(at * nk, sub * nk), sub * nk)
        z = z_ref[rng].astype(F32).reshape(-1, chan)
        hat, inverse = normalize(z)
        u = (hat * norms[0:1] + norms[1:2]).astype(LOW)
        ulow[flat] = u
        p = dot(u, proj[:, :4 * chan])
        m = row_mask(rowm.at[0], colm, at, sub)
        gl = gleft[rng].astype(F32).reshape(-1, chan) * m
        gr = (keep[rng].astype(F32) + got[rng].astype(F32)).reshape(-1, chan) * m
        for n, grad in ((0, gl), (2, gr)):
            sig = sigmoid(p[:, (n + 1) * chan:(n + 2) * chan])
            first = grad * sig
            plow[flat, n * chan:(n + 1) * chan] = first.astype(LOW)
            second = first * (p[:, n * chan:(n + 1) * chan] * (1.0 - sig))
            plow[flat, (n + 1) * chan:(n + 2) * chan] = second.astype(LOW)
        plow[flat, 4 * chan:] = gate_grad[rng].reshape(-1, chan)
        gu = dot(plow[flat], proj[...], 1, 1)
        nin[0] += eights(gu * hat)
        nin[1] += eights(gu)
        g = g_ref[rng].astype(F32).reshape(-1, chan)
        grad_z = g + norm_back(gu * norms[0:1], hat, inverse)
        out[rng] = grad_z.astype(LOW).reshape(sub, nk, chan)
        return 0

    lax.fori_loop(0, rows // sub, step, 0, unroll=rows // sub)
    wproj[...] += dot(ulow[...], plow[...], 0, 0)


def input_call(z, g, gleft, keep, got, gate_grad, norms, proj, rowm, colm, nblocks, h, parts,
               micros, token):
    tokens = [] if token is None else [token]
    ni, nk, chan = z.shape
    nrow = ni // nblocks
    rows = nrow // 4
    sub = rows // 2
    per = 4 // parts
    flat = pl.BlockSpec((rows, nk, chan), lambda s, r: (s * 4 + h * per + r, 0, 0))
    mask = pl.BlockSpec((1, rows, chan), lambda s, r: (s * 4 + h * per + r, 0, 0))
    rowm = rowm.reshape(-1, rows, chan)
    width = proj.shape[1]
    sums = [sds((chan, width), F32), sds((2, 8, chan), F32)]
    whole = lambda v: pl.BlockSpec(v.shape, lambda s, r: (0,) * len(v.shape))
    return pl.pallas_call(
        lambda *refs: input_kernel(sub, *refs[:10], *refs[10 + len(tokens):]),
        grid=(nblocks, per),
        in_specs=[flat] * 6 + [whole(norms), whole(proj), mask, whole(colm)]
        + [pl.BlockSpec(memory_space=pl.ANY)] * len(tokens),
        out_specs=[pl.BlockSpec((rows, nk, chan), lambda s, r: (s * per + r, 0, 0))]
        + [whole(v) for v in sums],
        out_shape=[sds((ni // parts, nk, chan), LOW)] + sums,
        scratch_shapes=[pltpu.VMEM((rows * nk, chan), LOW), pltpu.VMEM((rows * nk, width), LOW)],
        compiler_params=params(58),
        cost_estimate=cost(micros),
        name="input_grad",
    )(z, g, gleft, keep, got, gate_grad, norms, proj, rowm, colm, *tokens)


def place_call(blocks, b, batches, h, parts, whole=None):
    count, size, nk, chan = blocks.shape

    def kernel(*refs):
        refs[-2][...] = refs[0][...]
        refs[-1][...] = jnp.zeros_like(refs[-1])

    args = [blocks] + ([] if whole is None else [whole])
    return pl.pallas_call(
        kernel,
        grid=(count, 2),
        in_specs=[pl.BlockSpec((1, size // 2, nk, chan), lambda g, r: (g, r, 0, 0))]
        + [pl.BlockSpec(memory_space=pl.ANY)] * (len(args) - 1),
        out_specs=[pl.BlockSpec((1, size // 2, nk, chan),
                                lambda g, r: (b * count + g, h * 2 + r, 0, 0)),
                   pl.BlockSpec((8, 128), lambda g, r: (0, 0))],
        out_shape=[sds((count * batches, size * parts, nk, chan), LOW), sds((8, 128), F32)],
        input_output_aliases={} if whole is None else {1: 0},
        compiler_params=params(58),
        cost_estimate=cost(0.02),
        name="place",
    )(*args)


def shards(rows, cols, pair, cotangent, residue_mask, weights, norm_params, momentum,
           norm_momentum, average, norm_average):
    zeds = rows // 2
    crops, nrow, ncol, chan = pair.shape
    batches = crops // zeds
    length = residue_mask.shape[1]
    ni = zeds * nrow
    row = lax.axis_index("row")
    col = lax.axis_index("col")
    zed, core = row // 2, row % 2
    weight_low = weights.astype(LOW)
    project_low = jnp.concatenate([weight_low[n] for n in range(5)], axis=1)
    mask_float = residue_mask.astype(F32)
    by_column = jnp.stack([core] + list(range(cols))).astype(jnp.int32)
    by_distance = jnp.stack([core] + [col ^ e for e in range(cols)]).astype(jnp.int32)
    near = [b for b in range(batches - 1) if cols == 4]
    same_core = [[2 * q + c for q in range(zeds)] for c in range(2)]

    def zswap(blocks):
        return lax.all_to_all(blocks, "row", 0, 0, tiled=True, axis_index_groups=same_core)

    def coreswap(block):
        return lax.ppermute(block, "row", [(r, r ^ 1) for r in range(rows)])

    def after(values, *others):
        return lax.optimization_barrier((values, others))[0]

    def flat(v):
        return v.reshape(ni, ncol, chan)

    def blocked(v):
        return v.reshape(zeds, nrow, ncol, chan)

    def col_move(v, e):
        return lax.ppermute(v, "col", [(q, q ^ e) for q in range(cols)])

    def gather_near(own):
        return [own, col_move(own, 1), col_move(own, 2)]

    def gather_far(near):
        own, from_x, from_y = near
        half = own.shape[0] // 2
        return near + [col_move(from_y[:half], 1), col_move(from_x[half:], 2)]

    def sum_col(term):
        count = term.shape[0] // 2
        mine = lax.dynamic_slice_in_dim(term, core * count, count, 0)
        mine = mine + coreswap(lax.dynamic_slice_in_dim(term, (1 - core) * count, count, 0))
        step = 1
        while step < cols:
            mine = mine + lax.ppermute(mine, "col", [(q, q ^ step) for q in range(cols)])
            step *= 2
        return mine

    def sum_zed(mine, second, third):
        step = 2
        while step < rows:
            if step * 2 >= rows:
                mine = mine + second[:1]
            mine = mine + lax.ppermute(mine, "row", [(r, r ^ step) for r in range(rows)])
            step *= 2
        mine = mine + third[:1]
        got = coreswap(mine)
        return jnp.concatenate([jnp.where(core == 0, mine, got), jnp.where(core == 0, got, mine)])

    masks = []
    for b in range(batches):
        crop_mask = lax.dynamic_index_in_dim(mask_float, b * zeds + zed, 0, keepdims=False)
        by_block = crop_mask.reshape(zeds, 2, nrow)
        rowm = lax.dynamic_index_in_dim(by_block, core, 1, keepdims=False).reshape(-1)
        colm = lax.dynamic_slice_in_dim(crop_mask, col * ncol, ncol, 0)
        masks.append((jnp.broadcast_to(rowm[:, None], (ni, chan)),
                      jnp.broadcast_to(colm[:, None], (ncol, chan))))

    def take(whole, b):
        return whole[b * zeds:(b + 1) * zeds]

    def edges(b):
        left, right = edges_call(pairs[b], norm_params, project_low[:, :4 * chan], *masks[b])
        return left, right, coreswap(right)

    pairs, cots, kept, reduced = [], [], [], []
    last = None
    for b in range(batches):
        block = take(after(pair, block), b) if b else take(pair, b)
        last = zswap(after(block, last) if b else block)
        pairs.append(flat(last))
    sliced = [take(cotangent, b) for b in range(batches)]
    pairs[0] = after(pairs[0], sliced)
    for b in range(batches):
        last = zswap(after(sliced[b], last))
        cots.append(flat(last))
    for b in range(batches):
        if b:
            pairs[b] = after(pairs[b], part)
        left, right, other = edges(b)
        kept.append((left, right, other))
        part = product_call(by_column, left, right, other, cols, 33 if b else 3)
        ready = after(part, reduced[b - 1], cots[b - 1]) if b else part
        reduced.append(flat(lax.psum_scatter(ready, "col", scatter_dimension=0, tiled=True)))
    def collect(pieces, whole=None):
        token = None
        for blocks, b, h, share in pieces:
            whole, token = place_call(blocks, b, batches, h, share, whole)
        return whole, token

    gathered, news, gates, sums = [], [], [], []
    for b in range(batches):
        new, gx, gate_grad, wout, nout = middle_call(
            pairs[b], cots[b], reduced[b], norm_params, weight_low[4], weight_low[5])
        last = zswap(after(blocked(new), last))
        news.append((last, b, 0, 1))
        ready = after(gx, (gathered[b - 1], last) if b else reduced[-1])
        if b - 1 in near:
            gathered[b - 1] = gather_far(after(gathered[b - 1], gx, news[b - 1][0]))
            ready = after(gx, gathered[b - 1], last)
        if b in near:
            gathered.append(gather_near(ready))
        else:
            gathered.append([lax.all_gather(ready, "col", axis=0)])
        gates.append(gate_grad)
        sums.append((wout, nout))
    new_pair, placed = collect(news)
    term, earlier = 0.0, []
    for b in range(batches):
        final = b == batches - 1
        wout, nout = sums[b]
        grad = after(gathered[b], out) if b else gathered[b]
        if b in near and final:
            grad = gather_far(grad)
        gleft, keep, send = edge_grad_call(by_distance if b in near else by_column, *kept[b], grad, placed if b else None)
        got = coreswap(send)
        if b:
            got = after(got, last)
        share = 2 if final else 1
        backs = []
        for h in range(share):
            out = input_call(pairs[b], cots[b], gleft, keep, got, gates[b], norm_params,
                             project_low, *masks[b], zeds, h, share, 27 if final else 5,
                             None)
            back, wproj, nin = out
            wproj = jnp.transpose(wproj.reshape(chan, 5, chan), (1, 0, 2)).reshape(5 * chan, chan)
            part = [wproj, jnp.zeros_like(wout) if h else wout, jnp.sum(nin, axis=1),
                    jnp.zeros((2, chan), F32) if h else jnp.sum(nout, axis=1)]
            term = term + jnp.concatenate(part, axis=0)
            back = back.reshape(zeds, nrow // share, ncol, chan)
            if final and h == share - 1:
                term = sum_col(term)
                back = after(back, term)
            last = zswap(after(back, last))
            backs.append((last, b, h, share))
        if not final:
            earlier += backs
    pair_grad, second = collect(earlier + backs[:1])
    pair_grad, third = collect(backs[1:], pair_grad)
    grads = sum_zed(after(term, backs[0][0]), second, third)
    grad_weights = grads[: 6 * chan].reshape(weights.shape)
    grad_norms = grads[6 * chan:]
    rate = 0.1 / (length * math.sqrt(crops))
    new_momentum = MOMENT * momentum + grad_weights
    new_weights = weights - rate * (grad_weights + MOMENT * new_momentum)
    new_average = DECAY * average + (1.0 - DECAY) * new_weights
    new_norm_momentum = MOMENT * norm_momentum + grad_norms
    new_norms = norm_params - rate * (grad_norms + MOMENT * new_norm_momentum)
    new_norm_average = DECAY * norm_average + (1.0 - DECAY) * new_norms
    return (new_pair, pair_grad, new_weights, new_momentum, new_average, new_norms,
            new_norm_momentum, new_norm_average)


def solution(mesh):
    rows, cols = mesh.shape["row"], mesh.shape["col"]
    tiled = P(None, "row", "col", None)

    def body(*args):
        return shards(rows, cols, *args)

    return jax.shard_map(
        body,
        mesh=mesh,
        in_specs=(tiled, tiled) + (P(),) * 7,
        out_specs=(tiled, tiled) + (P(),) * 6,
        check_vma=False,
    )
```
